128 devices in a mesh: tok: 32 (over z, y, core), pb: 4 (over x).
Axes of the slice: x: 4, y: 4, z: 4, core: 2. Of those that a mesh axis runs over, the one named last changes fastest.
Arguments:
- activations: bfloat16 [65536, 14336], P('tok', 'pb'), may hold values from -6 to 6
- out_grads: bfloat16 [65536, 4096], P('tok', 'pb'), may hold values from -6 to 6
- proj_in: bfloat16 [14336, 64], P('pb'), may hold values from -0.046875 to 0.046875
- proj_out: bfloat16 [4096, 64], P('pb'), may hold values from -0.09375 to 0.09375
- doc_starts: int32 [512], replicated, may hold values from 0 to 65535, as said below
- doc_owner: int32 [512], replicated, may hold values from 0 to 31, as said below
- queries: bfloat16 [8192, 4096], P('pb', 'tok'), may hold values from -6 to 6
Outputs:
- scores: float32 [512, 8192], P('tok', 'pb')
The draws below stay inside these ranges and needn't reach their ends.
Inputs may be any that keep to these rules, and one draw needn't show every extreme that they name: doc_starts[0] is 0 and the offsets rise strictly; document d holds tokens doc_starts[d] to doc_starts[d+1] - 1, the last one up to 65535, and the last document is the single token 65535; no document but the first starts at a multiple of 512; the tokens of one aligned block of 512 belong to at most 9 documents, and in some block to exactly 9. `doc_owner`: the documents form runs of 32 consecutive ones starting at multiples of 32, each run naming every owner index once, and the last document of a run has the owner of the first document of the next run; among the documents with tokens in one aligned block of 512 tokens at most 2 have one owner, and in some block exactly 2.
All inputs are finite; a program needn't handle non-finite values.
Results may differ from the reference program's by a relative error of at most 0.013.
Values may be sent and summed in bfloat16 or wider, within the bound.
A program may use at most 128 MiB of HBM per device.

```python
import jax
import jax.numpy as jnp
from jax import lax

D = 4096
FF = 14336
R = 64
DOC_DEV = 16
Q = 8192
WIN = 9
SHARE = 512
OWNERS = 32
TOKENS = 65536
DOCS = 512


def draw_doc_starts(key, part):
    key = jax.random.fold_in(key, 11)
    key_heavy, key_slots, key_offsets = jax.random.split(key, 3)
    block_count = TOKENS // SHARE
    inner_slots = WIN - 1
    heavy_block = jax.random.randint(key_heavy, (), 0, block_count, dtype=jnp.int32)
    slot_grid = jax.random.permutation(key_slots, block_count * inner_slots).astype(jnp.int32).reshape(block_count, inner_slots)
    block_ids = jnp.arange(block_count, dtype=jnp.int32)
    slot_ids = jnp.arange(inner_slots, dtype=jnp.int32)
    forced = (block_ids[:, None] == heavy_block) | (block_ids[:, None] == block_count - 1) & (slot_ids[None, :] == 0)
    priority = jnp.where(forced, slot_grid - block_count * inner_slots, slot_grid).reshape(-1)
    slot_order = jnp.argsort(jnp.argsort(priority))
    chosen = (slot_order < DOCS - 1).reshape(block_count, inner_slots)
    counts = jnp.sum(chosen.astype(jnp.int32), axis=1)
    offsets = jnp.arange(SHARE, dtype=jnp.int32)
    scores = jax.random.randint(key_offsets, (block_count, SHARE), 0, 65536, dtype=jnp.int32) * SHARE + offsets[None, :]
    last_pick = (block_ids[:, None] == block_count - 1) & (offsets[None, :] == SHARE - 1)
    scores = jnp.where(last_pick, -1, scores)
    scores = jnp.where(offsets[None, :] == 0, 65536 * SHARE, scores)
    offset_order = jnp.argsort(jnp.argsort(scores, axis=1), axis=1)
    picked = offset_order < counts[:, None]
    picked = picked.at[0, 0].set(True)
    starts = jnp.nonzero(picked.reshape(-1), size=DOCS)[0]
    return starts.astype(jnp.int32)


def draw_doc_owner(key, part):
    key = jax.random.fold_in(key, 12)
    key_link, key_steps, key_order = jax.random.split(key, 3)
    run_count = DOC_DEV
    first_link = jax.random.randint(key_link, (1,), 0, OWNERS, dtype=jnp.int32)
    link_steps = jax.random.randint(key_steps, (run_count,), 1, OWNERS, dtype=jnp.int32)
    link_values = (first_link + jnp.cumsum(link_steps).astype(jnp.int32)) % OWNERS
    head_values = jnp.concatenate([first_link, link_values[:-1]])
    owner_values = jnp.arange(OWNERS, dtype=jnp.int32)
    scores = jax.random.randint(key_order, (run_count, OWNERS), 0, 65536, dtype=jnp.int32) * OWNERS + owner_values[None, :] + OWNERS
    scores = jnp.where(owner_values[None, :] == head_values[:, None], 0, scores)
    scores = jnp.where(owner_values[None, :] == link_values[:, None], 65536 * OWNERS + OWNERS, scores)
    return jnp.argsort(scores, axis=1).reshape(-1).astype(jnp.int32)


def shard_levels(key, dims, cuts, smallest, high):
    def one(axis_at, parts):
        heights = jax.random.uniform(jax.random.fold_in(jax.random.fold_in(key, 6), axis_at), (parts,), jnp.float32, smallest / len(cuts), high / len(cuts))
        return jnp.repeat(jnp.exp(heights), dims[axis_at] // parts).reshape((-1,) + (1,) * (len(dims) - axis_at - 1))

    factor_of = one(*cuts[0])
    for cut in cuts[1:]:
        factor_of = factor_of * one(*cut)
    return factor_of


def noise(key, extent, deviation, reach, pieces=(), kind=jnp.bfloat16):
    values = deviation * jax.random.normal(key, extent, jnp.float32)
    if pieces:
        values = values * shard_levels(key, extent, pieces, -0.22, 0.18)
    return jnp.clip(values, -reach, reach).astype(kind)


def setup_inputs(seed: int = 0) -> dict:
    splits = jax.random.split(jax.random.key(seed), 8)
    return {
        "activations": noise(splits[0], (TOKENS, FF), 1.0, 6.0, ((0, 32), (1, 4))),
        "out_grads": noise(splits[1], (TOKENS, D), 1.0, 6.0, ((0, 32), (1, 4))),
        "proj_in": noise(splits[2], (FF, R), FF ** -0.5, 0.046875, ((0, 4),)),
        "proj_out": noise(splits[3], (D, R), D ** -0.5, 0.09375, ((0, 4),)),
        "doc_starts": draw_doc_starts(jax.random.fold_in(splits[7], 71), 0),
        "doc_owner": draw_doc_owner(jax.random.fold_in(splits[7], 71), 0),
        "queries": noise(splits[6], (Q, R * R), 1.0, 6.0, ((0, 4), (1, 32))),
    }


EPS = 1e-06

def doc_ranks(doc_owner, per_owner):
    doc_count = doc_owner.shape[0]
    doc_order = jnp.arange(doc_count, dtype=jnp.int32)
    same_owner = (doc_owner[None, :] == doc_owner[:, None]) & (doc_order[None, :] < doc_order[:, None])
    return doc_owner * per_owner + lax.optimization_barrier(jnp.sum(same_owner.astype(jnp.int32), axis=1))

def reference(activations, out_grads, proj_in, proj_out, doc_starts, doc_owner, queries):
    act_proj = jnp.dot(activations, proj_in, preferred_element_type=jnp.float32).astype(jnp.bfloat16)
    grad_proj = jnp.dot(out_grads, proj_out, preferred_element_type=jnp.float32).astype(jnp.bfloat16)
    block_count = TOKENS // SHARE
    positions = jnp.arange(TOKENS, dtype=jnp.int32).reshape(block_count, SHARE)
    act_blocks = act_proj.reshape(block_count, SHARE, R)
    grad_blocks = grad_proj.reshape(block_count, SHARE, R)

    def add_block(totals, inputs):
        act_blk, grad_blk, pos_blk = inputs
        doc_index = lax.optimization_barrier(jnp.sum((doc_starts[None, :] <= pos_blk[:, None]).astype(jnp.int32), axis=1)) - 1
        outer_rows = (grad_blk.astype(jnp.float32)[:, :, None] * act_blk.astype(jnp.float32)[:, None, :]).reshape(SHARE, R * R)
        return (totals.at[doc_index].add(outer_rows), None)
    doc_grads, _ = lax.scan(add_block, jnp.zeros((DOCS, R * R), jnp.float32), (act_blocks, grad_blocks, positions))
    doc_rank = doc_ranks(doc_owner, DOC_DEV)
    ordered = jnp.zeros_like(doc_grads).at[doc_rank].set(doc_grads)
    norm_sizes = jnp.sqrt(lax.optimization_barrier(jnp.sum(ordered * ordered, axis=1, keepdims=True)) + EPS)
    unit_rows = (ordered / norm_sizes).astype(jnp.bfloat16)
    return jnp.dot(unit_rows, queries.T, preferred_element_type=jnp.float32)
```

```python
import functools

import jax
import jax.numpy as jnp
from jax import lax
from jax.experimental import pallas as pl
from jax.experimental.pallas import tpu as pltpu
from jax.sharding import PartitionSpec as P

EPS = 1e-06
SHARE = 512
SLOTS = 16
SUB = 256
MESH = pl.DeviceIdType.MESH
HOPS = (2, 1, 3, 0)
NT = (((1,), (1,)), ((), ()))
F32 = jnp.float32
BF16 = jnp.bfloat16


def remote(src, dst, send_sem, recv_sem, tok, pb):
    return pltpu.make_async_remote_copy(
        src_ref=src,
        dst_ref=dst,
        send_sem=send_sem,
        recv_sem=recv_sem,
        device_id=(tok, pb),
        device_id_type=MESH,
    )


def kernel(
    act_hbm,
    grad_hbm,
    win_hbm,
    wout_hbm,
    starts_ref,
    owner_ref,
    q_hbm,
    out_ref,
    act_buf,
    grad_buf,
    win,
    wout,
    proj_send,
    proj_own,
    proj_recv,
    proj_t,
    onehot_ref,
    place,
    lhs,
    wnd,
    wnd_recv,
    part_send,
    part_recv,
    units,
    va,
    vb,
    qa,
    qb,
    fa,
    fb,
    fa_recv,
    fb_recv,
    load_sem,
    w_sem,
    q_sem,
    qs_send,
    qs_recv,
    p_send,
    p_recv,
    w_send,
    w_recv,
    x_send,
    x_recv,
    u_send,
    u_recv,
    f_send,
    f_recv,
):
    tok = lax.axis_index("tok")
    pb = lax.axis_index("pb")
    z, y, c = tok // 8, (tok // 2) % 4, tok % 2
    steps = act_buf.shape[0]
    per_hop = steps // 4

    loads = [
        pltpu.make_async_copy(win_hbm, win, w_sem.at[0]),
        pltpu.make_async_copy(wout_hbm, wout, w_sem.at[1]),
    ]
    for copy in loads:
        copy.start()
    for s in range(steps):
        row = ((pb + HOPS[s // per_hop]) % 4) * SHARE + (s % per_hop) * SUB
        rows = pl.ds(pl.multiple_of(row, SUB), SUB)
        pltpu.make_async_copy(act_hbm.at[rows], act_buf.at[s], load_sem.at[0, s]).start()
        pltpu.make_async_copy(grad_hbm.at[rows], grad_buf.at[s], load_sem.at[1, s]).start()
        if s == 1:
            pltpu.make_async_copy(q_hbm.at[pl.ds(0, 1024)], qa.at[y], q_sem.at[0]).start()
            pltpu.make_async_copy(q_hbm.at[pl.ds(1024, 1024)], qb.at[z], q_sem.at[1]).start()

    barrier = pltpu.get_barrier_semaphore()
    for n in range(1, 4):
        pl.semaphore_signal(barrier, inc=1, device_id=(tok, (pb + n) % 4), device_id_type=MESH)

    @pl.loop(1, 32)
    def _(n):
        pl.semaphore_signal(barrier, inc=1, device_id=((tok + n) % 32, pb), device_id_type=MESH)

    token = (tok * 4 + pb) * SHARE
    starts = starts_ref[...]
    begun = starts <= token + lax.broadcasted_iota(jnp.int32, (SHARE, 512), 0)
    doc_lane = lax.broadcasted_iota(jnp.int32, (SLOTS, 512), 1)
    slot_row = lax.broadcasted_iota(jnp.int32, (SLOTS, 512), 0)
    enters = (doc_lane % SLOTS == slot_row).astype(F32)
    leaves = ((doc_lane > 0) & ((doc_lane + SLOTS - 1) % SLOTS == slot_row)).astype(F32)
    onehot_ref[...] = lax.dot_general(
        (enters - leaves).astype(BF16), begun.astype(F32).astype(BF16), NT, preferred_element_type=F32
    )
    lane8 = lax.broadcasted_iota(jnp.int32, (8, 512), 1)
    row8 = lax.broadcasted_iota(jnp.int32, (8, 512), 0)
    first = jnp.broadcast_to(starts, (8, 512)) // SHARE
    last = jnp.where(lane8 == 511, 127, pltpu.roll(first, 511, 1))
    facts = jnp.where(row8 == 0, first, jnp.where(row8 == 1, last, lane8 % SLOTS))
    rank = owner_ref[...] * 16 + lax.broadcasted_iota(jnp.int32, (1, 512), 1) // 32
    perm = (rank == lax.broadcasted_iota(jnp.int32, (512, 512), 0)).astype(F32).astype(BF16)
    ranked = lax.dot_general(perm, facts.astype(F32).astype(BF16), NT, preferred_element_type=F32)
    col = lax.broadcasted_iota(jnp.int32, (512, 512), 1)
    block = ((col // SLOTS) * 4 + pb).astype(F32)
    slot = (col % SLOTS).astype(F32)
    inside = (ranked[:, 0:1] <= block) & (block <= ranked[:, 1:2]) & (ranked[:, 2:3] == slot)
    place[...] = inside.astype(F32).astype(BF16)

    pl.semaphore_wait(barrier, 34)

    for h in range(2):
        pltpu.make_async_copy(q_hbm.at[pl.ds(0, 1024)], qa.at[0], q_sem.at[h]).wait()
    q_copies = []
    for n in range(1, 4):
        to_y = z * 8 + ((y + n) % 4) * 2 + c
        to_z = ((z + n) % 4) * 8 + y * 2 + c
        q_copies.append(remote(qa.at[y], qa.at[y], qs_send.at[0, n - 1], qs_recv.at[0, n - 1], to_y, pb))
        q_copies.append(remote(qb.at[z], qb.at[z], qs_send.at[1, n - 1], qs_recv.at[1, n - 1], to_z, pb))
    for copy in q_copies:
        copy.start()

    for copy in loads:
        copy.wait()

    @pl.loop(0, steps)
    def _(s):
        pltpu.make_async_copy(act_hbm.at[pl.ds(0, SUB)], act_buf.at[s], load_sem.at[0, s]).wait()
        pltpu.make_async_copy(grad_hbm.at[pl.ds(0, SUB)], grad_buf.at[s], load_sem.at[1, s]).wait()
        both = jnp.concatenate(
            [
                jnp.dot(act_buf[s], win[...], preferred_element_type=F32),
                jnp.dot(grad_buf[s], wout[...], preferred_element_type=F32),
            ],
            axis=1,
        )

        @pl.when(s < 3 * per_hop)
        def _():
            proj_send[s] = both.astype(BF16)
            q = s // per_hop
            hop = jnp.where(q == 0, HOPS[0], jnp.where(q == 1, HOPS[1], HOPS[2]))
            remote(
                proj_send.at[s], proj_recv.at[s], p_send.at[s], p_recv.at[s], tok, (pb + hop) % 4
            ).start()

        @pl.when(s >= 3 * per_hop)
        def _():
            proj_own[s - 3 * per_hop] = both

    proj_copies = [
        remote(proj_send.at[s], proj_recv.at[s], p_send.at[s], p_recv.at[s], tok, (pb + HOPS[s // per_hop]) % 4)
        for s in range(3 * per_hop)
    ]
    for copy in proj_copies:
        copy.wait_recv()
    sums = []
    for h in range(per_hop):
        total = proj_own[h]
        for q in range(3):
            total = total + proj_recv[q * per_hop + h].astype(F32)
        sums.append(total)
    proj = jnp.concatenate(sums, axis=0).astype(BF16).astype(F32)

    proj_t[...] = proj.T[64:128, :]
    onehot = onehot_ref[...]
    for r in range(64):
        picked = onehot * proj_t[r : r + 1, :]
        lhs[pl.ds((r // 2) * SLOTS, SLOTS), pl.ds((r % 2) * SHARE, SHARE)] = picked.astype(BF16)
    low = lax.broadcasted_iota(jnp.int32, (SHARE, 128), 1) < 64
    rhs = jnp.concatenate(
        [jnp.where(low, proj, 0.0), jnp.where(low, 0.0, pltpu.roll(proj, 64, 1))], axis=0
    ).astype(BF16)
    wnd[...] = jnp.dot(lhs[...], rhs, preferred_element_type=F32).astype(BF16)

    @pl.loop(1, 32)
    def _(n):
        to = (tok + n) % 32
        remote(
            wnd.at[pl.ds(pl.multiple_of(to * SLOTS, SLOTS), SLOTS)],
            wnd_recv.at[pl.ds(pl.multiple_of(tok * SLOTS, SLOTS), SLOTS)],
            w_send,
            w_recv,
            to,
            pb,
        ).start()

    mine = pl.ds(pl.multiple_of(tok * SLOTS, SLOTS), SLOTS)
    wnd_recv[mine, :] = wnd[mine, :]
    others = pl.ds(0, 31 * SLOTS)
    pltpu.make_async_copy(wnd_recv.at[others], wnd_recv.at[others], w_recv).wait()
    part = jnp.dot(place[...], wnd_recv[...], preferred_element_type=F32)
    part_send[...] = part.astype(BF16)
    x_copies = [
        remote(part_send, part_recv.at[n - 1], x_send.at[n - 1], x_recv.at[n - 1], tok, (pb + n) % 4)
        for n in range(1, 4)
    ]
    for copy in x_copies:
        copy.start()
    for copy in x_copies:
        copy.wait_recv()
    for n in range(3):
        part = part + part_recv[n].astype(F32)
    units[...] = part.astype(BF16).reshape(4, 4, 32, 128)

    u_copies = []
    for n in range(1, 4):
        ty, tz = (y + n) % 4, (z + n) % 4
        u_copies.append(
            remote(units.at[:, ty], va.at[y], u_send.at[0, n - 1], u_recv.at[0, n - 1], z * 8 + ty * 2 + c, pb)
        )
        u_copies.append(
            remote(units.at[tz], vb.at[z], u_send.at[1, n - 1], u_recv.at[1, n - 1], tz * 8 + y * 2 + c, pb)
        )
    for copy in u_copies:
        copy.start()
    va[y] = units[:, y]
    vb[z] = units[z]
    for copy in q_copies:
        copy.wait_recv()

    def scores(v, q):
        total = jnp.zeros((128, 1024), F32)
        for n in range(4):
            total = total + lax.dot_general(v[n].reshape(128, 128), q[n], NT, preferred_element_type=F32)
        return total.astype(BF16)

    for copy in u_copies[0::2]:
        copy.wait_recv()
    fa[:, :1024] = scores(va, qa)
    squares = jnp.zeros((128, 128), F32)
    for n in range(4):
        v = va[n].reshape(128, 128).astype(F32)
        squares = squares + v * v
    square = jnp.broadcast_to(jnp.sum(squares, axis=1, keepdims=True), (128, 128))
    high = square.astype(BF16)
    rest = (square - high.astype(F32)).astype(BF16)
    fa[:, 1024:] = jnp.where(lax.broadcasted_iota(jnp.int32, (128, 128), 1) < 64, high.astype(F32), rest.astype(F32)).astype(
        BF16
    )
    fa_me, fb_me = z * 2 + c, y * 2 + c

    @pl.loop(1, 8)
    def _(n):
        to = (fa_me + n) % 8
        remote(
            fa.at[pl.ds(pl.multiple_of(to * 16, 16), 16)],
            fa_recv.at[fa_me],
            f_send.at[0],
            f_recv.at[0],
            (to // 2) * 8 + y * 2 + to % 2,
            pb,
        ).start()

    for copy in u_copies[1::2]:
        copy.wait_recv()
    fb[...] = scores(vb, qb)

    @pl.loop(1, 8)
    def _(n):
        to = (fb_me + n) % 8
        remote(
            fb.at[pl.ds(pl.multiple_of(to * 16, 16), 16)],
            fb_recv.at[fb_me],
            f_send.at[1],
            f_recv.at[1],
            z * 8 + to,
            pb,
        ).start()

    fa_recv[fa_me] = fa[pl.ds(pl.multiple_of(fa_me * 16, 16), 16), :]
    fb_recv[fb_me] = fb[pl.ds(pl.multiple_of(fb_me * 16, 16), 16), :]
    pltpu.make_async_copy(fa_recv.at[pl.ds(0, 7)], fa_recv.at[pl.ds(0, 7)], f_recv.at[0]).wait()
    total_a = jnp.zeros((16, 1152), F32)
    for n in range(8):
        total_a = total_a + fa_recv[n].astype(F32)
    tail = total_a[:, 1024:]
    norm = lax.rsqrt(tail + pltpu.roll(tail, 64, 1) + EPS)[:, 0:1]
    out_ref[:, :1024] = total_a[:, :1024] * norm
    pltpu.make_async_copy(fb_recv.at[pl.ds(0, 7)], fb_recv.at[pl.ds(0, 7)], f_recv.at[1]).wait()
    total_b = jnp.zeros((16, 1024), F32)
    for n in range(8):
        total_b = total_b + fb_recv[n].astype(F32)
    out_ref[:, 1024:] = total_b * norm

    for copy in q_copies + proj_copies + x_copies + u_copies:
        copy.wait_send()
    pltpu.make_async_copy(wnd.at[others], wnd.at[others], w_send).wait()
    pltpu.make_async_copy(fa.at[pl.ds(0, 112)], fa.at[pl.ds(0, 112)], f_send.at[0]).wait()
    pltpu.make_async_copy(fb.at[pl.ds(0, 112)], fb.at[pl.ds(0, 112)], f_send.at[1]).wait()


def per_device(activations, out_grads, proj_in, proj_out, doc_starts, doc_owner, queries):
    any_spec = pl.BlockSpec(memory_space=pl.ANY)
    vmem_spec = pl.BlockSpec(memory_space=pltpu.VMEM)
    depth_in, depth_out = activations.shape[1], out_grads.shape[1]
    steps = activations.shape[0] // SUB
    per_hop = steps // 4
    dma = pltpu.SemaphoreType.DMA
    return pl.pallas_call(
        kernel,
        out_shape=jax.ShapeDtypeStruct((16, 2048), F32),
        in_specs=[any_spec, any_spec, any_spec, any_spec, vmem_spec, vmem_spec, any_spec],
        out_specs=vmem_spec,
        scratch_shapes=[
            pltpu.VMEM((steps, SUB, depth_in), BF16),
            pltpu.VMEM((steps, SUB, depth_out), BF16),
            pltpu.VMEM((depth_in, 64), BF16),
            pltpu.VMEM((depth_out, 64), BF16),
            pltpu.VMEM((3 * per_hop, SUB, 128), BF16),
            pltpu.VMEM((per_hop, SUB, 128), F32),
            pltpu.VMEM((3 * per_hop, SUB, 128), BF16),
            pltpu.VMEM((64, SHARE), F32),
            pltpu.VMEM((SLOTS, SHARE), F32),
            pltpu.VMEM((512, 512), BF16),
            pltpu.VMEM((512, 2 * SHARE), BF16),
            pltpu.VMEM((512, 128), BF16),
            pltpu.VMEM((512, 128), BF16),
            pltpu.VMEM((512, 128), BF16),
            pltpu.VMEM((3, 512, 128), BF16),
            pltpu.VMEM((4, 4, 32, 128), BF16),
            pltpu.VMEM((4, 4, 32, 128), BF16),
            pltpu.VMEM((4, 4, 32, 128), BF16),
            pltpu.VMEM((4, 1024, 128), BF16),
            pltpu.VMEM((4, 1024, 128), BF16),
            pltpu.VMEM((128, 1152), BF16),
            pltpu.VMEM((128, 1024), BF16),
            pltpu.VMEM((8, 16, 1152), BF16),
            pltpu.VMEM((8, 16, 1024), BF16),
            dma((2, steps)),
            dma((2,)),
            dma((2,)),
            dma((2, 3)),
            dma((2, 3)),
            dma((3 * per_hop,)),
            dma((3 * per_hop,)),
            dma,
            dma,
            dma((3,)),
            dma((3,)),
            dma((2, 3)),
            dma((2, 3)),
            dma((2,)),
            dma((2,)),
        ],
        compiler_params=pltpu.CompilerParams(
            collective_id=0, has_side_effects=True, vmem_limit_bytes=52 * 1024 * 1024
        ),
    )(
        activations,
        out_grads,
        proj_in,
        proj_out,
        doc_starts.reshape(1, 512),
        doc_owner.reshape(1, 512),
        queries,
    )


def solution(mesh):
    in_specs = (
        P("tok", "pb"),
        P("tok", "pb"),
        P("pb", None),
        P("pb", None),
        P(),
        P(),
        P("pb", "tok"),
    )
    return jax.shard_map(
        per_device, mesh=mesh, in_specs=in_specs, out_specs=P("tok", "pb"), check_vma=False
    )
```

```python
import functools

import jax
import jax.numpy as jnp
from jax import lax
from jax.experimental import pallas as pl
from jax.experimental.pallas import tpu as pltpu
from jax.sharding import PartitionSpec as P

EPS = 1e-06
SHARE = 512
SLOTS = 16
MESH = pl.DeviceIdType.MESH
DEVICES = 128
NT = (((1,), (1,)), ((), ()))
F32 = jnp.float32
BF16 = jnp.bfloat16


def remote(src, dst, send_sem, recv_sem, tok, pb):
    return pltpu.make_async_remote_copy(
        src_ref=src,
        dst_ref=dst,
        send_sem=send_sem,
        recv_sem=recv_sem,
        device_id=(tok, pb),
        device_id_type=MESH,
    )


def hop_of(t):
    return jnp.where(t == 0, 2, jnp.where(t == 1, 1, jnp.where(t == 2, 3, 0)))


def kernel(
    act_hbm,
    grad_hbm,
    win_hbm,
    wout_hbm,
    starts_hbm,
    owner_hbm,
    q_hbm,
    out_ref,
    act_buf,
    grad_buf,
    win,
    wout,
    starts_ref,
    owner_ref,
    proj_send,
    proj_own,
    proj_recv,
    proj_t,
    onehot_ref,
    place,
    lhs,
    wnd,
    wnd_recv,
    units,
    va,
    vb,
    qa,
    qb,
    qa_t,
    qb_t,
    fa,
    fb,
    fa_recv,
    fb_recv,
    load_sem,
    w_sem,
    q_sem,
    qs_send,
    qs_recv,
    p_send,
    p_recv,
    d_send,
    d_recv,
    u_send,
    u_recv,
    f_send,
    f_recv,
):
    tok = lax.axis_index("tok")
    pb = lax.axis_index("pb")
    z, y, c = tok // 8, (tok // 2) % 4, tok % 2
    me = tok * 4 + pb

    def tile_loads(t):
        rows = pl.ds(pl.multiple_of(((pb + hop_of(t)) % 4) * SHARE, SHARE), SHARE)
        return [
            pltpu.make_async_copy(grad_hbm.at[rows], grad_buf.at[t], load_sem.at[0, t]),
            pltpu.make_async_copy(act_hbm.at[rows], act_buf.at[t], load_sem.at[1, t]),
        ]

    small = [
        pltpu.make_async_copy(wout_hbm, wout, w_sem.at[0]),
        pltpu.make_async_copy(win_hbm, win, w_sem.at[1]),
        pltpu.make_async_copy(starts_hbm, starts_ref, w_sem.at[2]),
        pltpu.make_async_copy(owner_hbm, owner_ref, w_sem.at[3]),
    ]
    q_loads = [
        pltpu.make_async_copy(q_hbm.at[pl.ds(0, 1024)], qa.at[y], q_sem.at[0]),
        pltpu.make_async_copy(q_hbm.at[pl.ds(1024, 1024)], qb.at[z], q_sem.at[1]),
    ]
    small[0].start()
    small[1].start()
    for copy in q_loads + tile_loads(0) + tile_loads(1):
        copy.start()
    small[2].start()
    small[3].start()

    barrier = pltpu.get_barrier_semaphore()

    planes = [lax.rem(pb + n, 4) for n in range(4)]
    for plane in planes[1:]:
        pl.semaphore_signal(barrier, inc=1, device_id=(tok, plane), device_id_type=MESH)

    @pl.loop(1, 32)
    def _(n):
        to = lax.rem(tok + n, 32)
        for plane in planes:
            pl.semaphore_signal(barrier, inc=1, device_id=(to, plane), device_id_type=MESH)

    q_copies = []
    for n in range(1, 4):
        to_y = z * 8 + ((y + n) % 4) * 2 + c
        to_z = ((z + n) % 4) * 8 + y * 2 + c
        q_copies.append(remote(qa.at[y], qa.at[y], qs_send.at[0, n - 1], qs_recv.at[0, n - 1], to_y, pb))
        q_copies.append(remote(qb.at[z], qb.at[z], qs_send.at[1, n - 1], qs_recv.at[1, n - 1], to_z, pb))

    pl.semaphore_wait(barrier, DEVICES - 1)
    for copy in q_loads:
        copy.wait()
    for copy in q_copies:
        copy.start()

    for copy in small[:2]:
        copy.wait()

    def proj_copy(t):
        return remote(
            proj_send.at[t], proj_recv.at[t], p_send.at[t], p_recv.at[t], tok, (pb + hop_of(t)) % 4
        )

    @pl.loop(0, 4)
    def _(t):
        @pl.when(t < 2)
        def _():
            for copy in tile_loads(t + 2):
                copy.start()

        for copy in tile_loads(t):
            copy.wait()
        both = jnp.concatenate(
            [
                lax.dot_general(act_buf[t], win[...], NT, preferred_element_type=F32),
                lax.dot_general(grad_buf[t], wout[...], NT, preferred_element_type=F32),
            ],
            axis=1,
        )

        @pl.when(t < 3)
        def _():
            proj_send[t] = both.astype(BF16)
            proj_copy(t).start()

        @pl.when(t == 3)
        def _():
            proj_own[...] = both

    for copy in small[2:]:
        copy.wait()
    starts = starts_ref[...]
    begun = starts <= me * SHARE + lax.broadcasted_iota(jnp.int32, (SHARE, 512), 0)
    doc_lane = lax.broadcasted_iota(jnp.int32, (SLOTS, 512), 1)
    slot_row = lax.broadcasted_iota(jnp.int32, (SLOTS, 512), 0)
    enters = (doc_lane % SLOTS == slot_row).astype(F32)
    leaves = ((doc_lane > 0) & ((doc_lane + SLOTS - 1) % SLOTS == slot_row)).astype(F32)
    onehot_ref[...] = lax.dot_general(
        (enters - leaves).astype(BF16), begun.astype(F32).astype(BF16), NT, preferred_element_type=F32
    )

    for t in range(3):
        proj_copy(t).wait_recv()
    proj = proj_own[...]
    for t in range(3):
        proj = proj + proj_recv[t].astype(F32)
    proj = proj.astype(BF16).astype(F32)

    proj_t[...] = proj.T[64:128, :]
    onehot = onehot_ref[...]
    for r in range(64):
        picked = onehot * proj_t[r : r + 1, :]
        lhs[pl.ds((r // 2) * SLOTS, SLOTS), pl.ds((r % 2) * SHARE, SHARE)] = picked.astype(BF16)
    low = lax.broadcasted_iota(jnp.int32, (SHARE, 128), 1) < 64
    rhs = jnp.concatenate(
        [jnp.where(low, proj, 0.0), jnp.where(low, 0.0, pltpu.roll(proj, 64, 1))], axis=0
    ).astype(BF16)
    wnd[...] = jnp.dot(lhs[...], rhs, preferred_element_type=F32).astype(BF16)

    mine = pl.ds(pl.multiple_of((me % 32) * SLOTS, SLOTS), SLOTS)

    def send_block(to, plane):
        remote(
            wnd.at[pl.ds(pl.multiple_of(to * SLOTS, SLOTS), SLOTS)],
            wnd_recv.at[z, mine],
            d_send,
            d_recv.at[z],
            to,
            plane,
        ).start()

    for plane in planes[1:]:
        send_block(tok, plane)

    @pl.loop(1, 32)
    def _(n):
        to = lax.rem(tok + n, 32)
        for plane in planes:
            send_block(to, plane)

    wnd_recv[z, mine, :] = wnd[pl.ds(pl.multiple_of(tok * SLOTS, SLOTS), SLOTS), :]

    lane8 = lax.broadcasted_iota(jnp.int32, (8, 512), 1)
    row8 = lax.broadcasted_iota(jnp.int32, (8, 512), 0)
    first = jnp.broadcast_to(starts, (8, 512)) // SHARE
    last = jnp.where(lane8 == 511, DEVICES - 1, pltpu.roll(first, 511, 1))
    facts = jnp.where(row8 == 0, first, jnp.where(row8 == 1, last, lane8 % SLOTS))
    rank = owner_ref[...] * 16 + lax.broadcasted_iota(jnp.int32, (1, 512), 1) // 32
    perm = (rank == lax.broadcasted_iota(jnp.int32, (512, 512), 0)).astype(F32).astype(BF16)
    ranked = lax.dot_general(perm, facts.astype(F32).astype(BF16), NT, preferred_element_type=F32)
    col = lax.broadcasted_iota(jnp.int32, (512, 512), 1)
    block = (col // SLOTS).astype(F32)
    own_slot = ranked[:, 2:3] == (col % SLOTS).astype(F32)

    @pl.loop(0, 4)
    def _(g):
        from_block = ranked[:, 0:1] - (g * 32).astype(F32)
        to_block = ranked[:, 1:2] - (g * 32).astype(F32)
        inside = (from_block <= block) & (block <= to_block) & own_slot
        place[g] = inside.astype(F32).astype(BF16)

    for copy in q_copies:
        copy.wait_recv()
    for n in range(4):
        qa_t[pl.ds(n * 128, 128), :] = qa[n].T
        qb_t[pl.ds(n * 128, 128), :] = qb[n].T

    summed = jnp.zeros((512, 128), F32)
    for n in (3, 2, 1, 0):
        g = (z + n) % 4
        got = wnd_recv.at[g, pl.ds(0, 512 if n else 496)]
        pltpu.make_async_copy(got, got, d_recv.at[g]).wait()
        summed = summed + jnp.dot(place[g], wnd_recv[g], preferred_element_type=F32)
    units[...] = summed.astype(BF16).reshape(4, 4, 32, 128)

    at_y = pl.ds(pl.multiple_of(y * 128, 128), 128)
    at_z = pl.ds(pl.multiple_of(z * 128, 128), 128)
    u_copies = []
    for n in range(1, 4):
        ty, tz = (y + n) % 4, (z + n) % 4
        u_copies.append(
            remote(
                units.at[tz], vb.at[:, :, at_z], u_send.at[1, n - 1], u_recv.at[1, n - 1], tz * 8 + y * 2 + c, pb
            )
        )
        u_copies.append(
            remote(
                units.at[:, ty], va.at[:, :, at_y], u_send.at[0, n - 1], u_recv.at[0, n - 1], z * 8 + ty * 2 + c, pb
            )
        )
    for copy in u_copies:
        copy.start()
    va[:, :, at_y] = units[:, y]
    vb[:, :, at_z] = units[z]
    fa_me, fb_me = z * 2 + c, y * 2 + c

    for copy in u_copies[0::2]:
        copy.wait_recv()
    fb[...] = jnp.dot(vb[...].reshape(128, 512), qb_t[...], preferred_element_type=F32).astype(BF16)

    @pl.loop(1, 8)
    def _(n):
        to = (fb_me + n) % 8
        remote(
            fb.at[pl.ds(pl.multiple_of(to * 16, 16), 16)],
            fb_recv.at[fb_me],
            f_send.at[1],
            f_recv.at[1],
            z * 8 + to,
            pb,
        ).start()

    for copy in u_copies[1::2]:
        copy.wait_recv()
    docs = va[...].reshape(128, 512)
    fa[:, :1024] = jnp.dot(docs, qa_t[...], preferred_element_type=F32).astype(BF16)
    wide = docs.astype(F32)
    square = jnp.broadcast_to(jnp.sum(wide * wide, axis=1, keepdims=True), (128, 128))
    high = square.astype(BF16).astype(F32)
    fa[:, 1024:] = jnp.where(
        lax.broadcasted_iota(jnp.int32, (128, 128), 1) < 64, high, square - high
    ).astype(BF16)

    @pl.loop(1, 8)
    def _(n):
        to = (fa_me + n) % 8
        remote(
            fa.at[pl.ds(pl.multiple_of(to * 16, 16), 16)],
            fa_recv.at[fa_me],
            f_send.at[0],
            f_recv.at[0],
            (to // 2) * 8 + y * 2 + to % 2,
            pb,
        ).start()

    fa_recv[fa_me] = fa[pl.ds(pl.multiple_of(fa_me * 16, 16), 16), :]
    fb_recv[fb_me] = fb[pl.ds(pl.multiple_of(fb_me * 16, 16), 16), :]
    pltpu.make_async_copy(fb_recv.at[pl.ds(0, 7)], fb_recv.at[pl.ds(0, 7)], f_recv.at[1]).wait()
    total_b = fb_recv[0].astype(F32)
    for n in range(1, 8):
        total_b = total_b + fb_recv[n].astype(F32)
    pltpu.make_async_copy(fa_recv.at[pl.ds(0, 7)], fa_recv.at[pl.ds(0, 7)], f_recv.at[0]).wait()
    total_a = fa_recv[0].astype(F32)
    for n in range(1, 8):
        total_a = total_a + fa_recv[n].astype(F32)
    tail = total_a[:, 1024:]
    norm = lax.rsqrt(tail + pltpu.roll(tail, 64, 1) + EPS)[:, 0:1]
    out_ref[:, :1024] = total_a[:, :1024] * norm
    out_ref[:, 1024:] = total_b * norm

    for t in range(3):
        proj_copy(t).wait_send()
    for copy in q_copies + u_copies:
        copy.wait_send()
    for g in range(4):
        some = wnd.at[pl.ds(0, 512 if g else 496)]
        pltpu.make_async_copy(some, some, d_send).wait()
    pltpu.make_async_copy(fa.at[pl.ds(0, 112)], fa.at[pl.ds(0, 112)], f_send.at[0]).wait()
    pltpu.make_async_copy(fb.at[pl.ds(0, 112)], fb.at[pl.ds(0, 112)], f_send.at[1]).wait()


def per_device(activations, out_grads, proj_in, proj_out, doc_starts, doc_owner, queries):
    depth_in, depth_out = activations.shape[1], out_grads.shape[1]
    dma = pltpu.SemaphoreType.DMA
    vmem = pltpu.VMEM

    def on_hbm(array):
        return pltpu.with_memory_space_constraint(array, pltpu.HBM)

    return pl.pallas_call(
        kernel,
        out_shape=jax.ShapeDtypeStruct((16, 2048), F32),
        in_specs=[pl.BlockSpec(memory_space=pltpu.HBM)] * 7,
        out_specs=pl.BlockSpec(memory_space=pltpu.VMEM),
        scratch_shapes=[
            vmem((4, SHARE, depth_in), BF16),
            vmem((4, SHARE, depth_out), BF16),
            vmem((64, depth_in), BF16),
            vmem((64, depth_out), BF16),
            vmem((1, 512), jnp.int32),
            vmem((1, 512), jnp.int32),
            vmem((3, SHARE, 128), BF16),
            vmem((SHARE, 128), F32),
            vmem((3, SHARE, 128), BF16),
            vmem((64, SHARE), F32),
            vmem((SLOTS, SHARE), F32),
            vmem((4, 512, 512), BF16),
            vmem((512, 2 * SHARE), BF16),
            vmem((512, 128), BF16),
            vmem((4, 512, 128), BF16),
            vmem((4, 4, 32, 128), BF16),
            vmem((4, 32, 512), BF16),
            vmem((4, 32, 512), BF16),
            vmem((4, 1024, 128), BF16),
            vmem((4, 1024, 128), BF16),
            vmem((512, 1024), BF16),
            vmem((512, 1024), BF16),
            vmem((128, 1152), BF16),
            vmem((128, 1024), BF16),
            vmem((8, 16, 1152), BF16),
            vmem((8, 16, 1024), BF16),
            dma((2, 4)),
            dma((4,)),
            dma((2,)),
            dma((2, 3)),
            dma((2, 3)),
            dma((3,)),
            dma((3,)),
            dma,
            dma((4,)),
            dma((2, 3)),
            dma((2, 3)),
            dma((2,)),
            dma((2,)),
        ],
        compiler_params=pltpu.CompilerParams(
            collective_id=0, has_side_effects=True, vmem_limit_bytes=48 * 1024 * 1024
        ),
    )(
        on_hbm(activations),
        on_hbm(out_grads),
        on_hbm(proj_in.T),
        on_hbm(proj_out.T),
        on_hbm(doc_starts.reshape(1, 512)),
        on_hbm(doc_owner.reshape(1, 512)),
        on_hbm(queries),
    )


def solution(mesh):
    in_specs = (
        P("tok", "pb"),
        P("tok", "pb"),
        P("pb", None),
        P("pb", None),
        P(),
        P(),
        P("pb", "tok"),
    )
    return jax.shard_map(
        per_device, mesh=mesh, in_specs=in_specs, out_specs=P("tok", "pb"), check_vma=False
    )
```

```python
import functools

import jax
import jax.numpy as jnp
from jax import lax
from jax.experimental import pallas as pl
from jax.experimental.pallas import tpu as pltpu
from jax.sharding import PartitionSpec as P

EPS = 1e-06
SHARE = 512
SLOTS = 16
MESH = pl.DeviceIdType.MESH
DEVICES = 128
HALF = 256
NT = (((1,), (1,)), ((), ()))
F32 = jnp.float32
BF16 = jnp.bfloat16


def remote(src, dst, send_sem, recv_sem, tok, pb):
    return pltpu.make_async_remote_copy(
        src_ref=src,
        dst_ref=dst,
        send_sem=send_sem,
        recv_sem=recv_sem,
        device_id=(tok, pb),
        device_id_type=MESH,
    )


def hop_of(t):
    return jnp.where(t == 0, 2, jnp.where(t == 1, 1, jnp.where(t == 2, 3, 0)))


def kernel(
    act_hbm,
    grad_hbm,
    win_hbm,
    wout_hbm,
    starts_hbm,
    owner_hbm,
    q_hbm,
    out_ref,
    act_buf,
    grad_buf,
    win,
    wout,
    starts_ref,
    owner_ref,
    proj_send,
    proj_own,
    proj_recv,
    proj_t,
    onehot_ref,
    place,
    lhs,
    rhs,
    wnd,
    wnd_recv,
    units,
    va,
    vb,
    qa,
    qb,
    qa_t,
    qb_t,
    fa,
    fb,
    fa_recv,
    fb_recv,
    load_sem,
    w_sem,
    q_sem,
    qs_send,
    qs_recv,
    p_send,
    p_recv,
    d_send,
    d_recv,
    u_send,
    u_recv,
    f_send,
    f_recv,
):
    tok = lax.axis_index("tok")
    pb = lax.axis_index("pb")
    z, y, c = tok // 8, (tok // 2) % 4, tok % 2
    me = tok * 4 + pb

    def loads_of(rows, t, at, sem):
        return [
            pltpu.make_async_copy(grad_hbm.at[rows], grad_buf.at[t, at], load_sem.at[0, sem]),
            pltpu.make_async_copy(act_hbm.at[rows], act_buf.at[t, at], load_sem.at[1, sem]),
        ]

    def half_of(s):
        return lax.rem(s, 3), pl.ds(pl.multiple_of(lax.div(s, 3) * HALF, HALF), HALF)

    def half_loads(s):
        t, at = half_of(s)
        start = lax.rem(pb + hop_of(t), 4) * SHARE + lax.div(s, 3) * HALF
        return loads_of(pl.ds(pl.multiple_of(start, HALF), HALF), t, at, s)

    own_loads = loads_of(pl.ds(pl.multiple_of(pb * SHARE, SHARE), SHARE), 3, pl.ds(0, SHARE), 6)
    small = [
        pltpu.make_async_copy(wout_hbm, wout, w_sem.at[0]),
        pltpu.make_async_copy(win_hbm, win, w_sem.at[1]),
        pltpu.make_async_copy(starts_hbm, starts_ref, w_sem.at[2]),
        pltpu.make_async_copy(owner_hbm, owner_ref, w_sem.at[3]),
    ]
    q_loads = [
        pltpu.make_async_copy(q_hbm.at[pl.ds(0, 1024)], qa.at[y], q_sem.at[0]),
        pltpu.make_async_copy(q_hbm.at[pl.ds(1024, 1024)], qb.at[z], q_sem.at[1]),
    ]
    small[0].start()
    small[1].start()
    for copy in half_loads(0) + q_loads:
        copy.start()

    @pl.loop(1, 6)
    def _(s):
        for copy in half_loads(s):
            copy.start()

    for copy in own_loads:
        copy.start()
    small[2].start()
    small[3].start()

    barrier = pltpu.get_barrier_semaphore()

    planes = [lax.rem(pb + n, 4) for n in range(4)]
    for plane in planes[1:]:
        pl.semaphore_signal(barrier, inc=1, device_id=(tok, plane), device_id_type=MESH)

    @pl.loop(1, 32)
    def _(n):
        to = lax.rem(tok + n, 32)
        for plane in planes:
            pl.semaphore_signal(barrier, inc=1, device_id=(to, plane), device_id_type=MESH)

    q_copies, q_passed = [], []
    for h, (q_all, place_me) in enumerate(((qa, y), (qb, z))):
        right, left = lax.rem(place_me + 1, 4), lax.rem(place_me + 3, 4)
        for k, (to, rows, src) in enumerate(
            (
                (right, pl.ds(0, 1024), place_me),
                (left, pl.ds(0, 1024), place_me),
                (right, pl.ds(0, 512), left),
                (left, pl.ds(512, 512), right),
            )
        ):
            part = q_all.at[src, rows]
            to_tok = z * 8 + to * 2 + c if h == 0 else to * 8 + y * 2 + c
            copy = remote(part, part, qs_send.at[h, k], qs_recv.at[h, k], to_tok, pb)
            (q_copies if k < 2 else q_passed).append(copy)

    for copy in small[:2]:
        copy.wait()

    def project(t, at):
        return jnp.concatenate(
            [
                lax.dot_general(act_buf[t, at, :], win[...], NT, preferred_element_type=F32),
                lax.dot_general(grad_buf[t, at, :], wout[...], NT, preferred_element_type=F32),
            ],
            axis=1,
        )

    def proj_copy(s):
        t, at = half_of(s)
        return remote(
            proj_send.at[t, at], proj_recv.at[t, at], p_send.at[s], p_recv.at[s], tok, lax.rem(pb + hop_of(t), 4)
        )

    @pl.loop(0, 6)
    def _(s):
        for copy in half_loads(s):
            copy.wait()
        t, at = half_of(s)
        proj_send[t, at, :] = project(t, at).astype(BF16)

        @pl.when(s == 0)
        def _():
            pl.semaphore_wait(barrier, DEVICES - 1)
            for copy in q_loads:
                copy.wait()
            for copy in q_copies:
                copy.start()

        proj_copy(s).start()

    for copy in own_loads:
        copy.wait()
    proj_own[...] = project(3, pl.ds(0, SHARE))
    proj_copies = [proj_copy(s) for s in range(6)]

    for copy in small[2:]:
        copy.wait()
    starts = starts_ref[...]
    begun = starts <= me * SHARE + lax.broadcasted_iota(jnp.int32, (SHARE, 512), 0)
    doc_lane = lax.broadcasted_iota(jnp.int32, (SLOTS, 512), 1)
    slot_row = lax.broadcasted_iota(jnp.int32, (SLOTS, 512), 0)
    enters = (doc_lane % SLOTS == slot_row).astype(F32)
    leaves = ((doc_lane > 0) & ((doc_lane + SLOTS - 1) % SLOTS == slot_row)).astype(F32)
    onehot_ref[...] = lax.dot_general(
        (enters - leaves).astype(BF16), begun.astype(F32).astype(BF16), NT, preferred_element_type=F32
    )

    for copy in proj_copies:
        copy.wait_recv()
    proj = proj_own[...]
    for t in range(3):
        proj = proj + proj_recv[t].astype(F32)
    proj = proj.astype(BF16).astype(F32)

    proj_t[...] = proj.T[64:128, :]
    onehot = onehot_ref[...]
    low = lax.broadcasted_iota(jnp.int32, (SHARE, 128), 1) < 64
    rhs[...] = jnp.concatenate(
        [jnp.where(low, proj, 0.0), jnp.where(low, 0.0, pltpu.roll(proj, 64, 1))], axis=0
    ).astype(BF16)
    mine = pl.ds(pl.multiple_of(lax.rem(me, 32) * SLOTS, SLOTS), SLOTS)
    far_planes = [planes[2], planes[1], planes[3], planes[0]]

    def send_block(to, plane):
        remote(
            wnd.at[pl.ds(pl.multiple_of(to * SLOTS, SLOTS), SLOTS)],
            wnd_recv.at[z, mine],
            d_send,
            d_recv.at[z],
            to,
            plane,
        ).start()

    @pl.loop(0, 4)
    def _(k):
        g = lax.rem(z + hop_of(k), 4)
        rows = proj_t[pl.ds(pl.multiple_of(g * 16, 16), 16), :]
        for r in range(16):
            picked = onehot * rows[r : r + 1, :]
            lhs[pl.ds((r // 2) * SLOTS, SLOTS), pl.ds((r % 2) * SHARE, SHARE)] = picked.astype(BF16)
        wnd[pl.ds(pl.multiple_of(g * 128, 128), 128), :] = jnp.dot(
            lhs[...], rhs[...], preferred_element_type=F32
        ).astype(BF16)

        @pl.loop(0, 3)
        def _(n):
            row = g * 8 + lax.rem(y + hop_of(n), 4) * 2
            for plane in far_planes:
                send_block(row + c, plane)
                send_block(row + 1 - c, plane)

        for plane in far_planes[:3]:
            send_block(g * 8 + y * 2 + c, plane)
            send_block(g * 8 + y * 2 + 1 - c, plane)
        send_block(g * 8 + y * 2 + 1 - c, pb)

        @pl.when(k < 3)
        def _():
            send_block(g * 8 + y * 2 + c, pb)

    wnd_recv[z, mine, :] = wnd[pl.ds(pl.multiple_of(tok * SLOTS, SLOTS), SLOTS), :]
    for copy in q_copies:
        copy.wait_recv()
    for copy in q_passed:
        copy.start()

    lane8 = lax.broadcasted_iota(jnp.int32, (8, 512), 1)
    row8 = lax.broadcasted_iota(jnp.int32, (8, 512), 0)
    first = jnp.broadcast_to(starts, (8, 512)) // SHARE
    last = jnp.where(lane8 == 511, DEVICES - 1, pltpu.roll(first, 511, 1))
    facts = jnp.where(row8 == 0, first, jnp.where(row8 == 1, last, lane8 % SLOTS))
    rank = owner_ref[...] * 16 + lax.broadcasted_iota(jnp.int32, (1, 512), 1) // 32
    perm = (rank == lax.broadcasted_iota(jnp.int32, (512, 512), 0)).astype(F32).astype(BF16)
    ranked = lax.dot_general(perm, facts.astype(F32).astype(BF16), NT, preferred_element_type=F32)
    col = lax.broadcasted_iota(jnp.int32, (512, 512), 1)
    block = (col // SLOTS).astype(F32)
    own_slot = ranked[:, 2:3] == (col % SLOTS).astype(F32)

    @pl.loop(0, 4)
    def _(g):
        from_block = ranked[:, 0:1] - (g * 32).astype(F32)
        to_block = ranked[:, 1:2] - (g * 32).astype(F32)
        inside = (from_block <= block) & (block <= to_block) & own_slot
        place[g] = inside.astype(F32).astype(BF16)

    summed = jnp.zeros((512, 128), F32)
    for n in (2, 3, 1, 0):
        g = (z + n) % 4
        got = wnd_recv.at[g, pl.ds(0, 512 if n else 496)]
        pltpu.make_async_copy(got, got, d_recv.at[g]).wait()
        summed = summed + jnp.dot(place[g], wnd_recv[g], preferred_element_type=F32)
    units[...] = summed.astype(BF16).reshape(4, 4, 32, 128)

    at_y = pl.ds(pl.multiple_of(y * 128, 128), 128)
    at_z = pl.ds(pl.multiple_of(z * 128, 128), 128)
    u_copies = []
    for n in range(1, 4):
        ty, tz = (y + n) % 4, (z + n) % 4
        u_copies.append(
            remote(
                units.at[tz], vb.at[:, :, at_z], u_send.at[1, n - 1], u_recv.at[1, n - 1], tz * 8 + y * 2 + c, pb
            )
        )
        u_copies.append(
            remote(
                units.at[:, ty], va.at[:, :, at_y], u_send.at[0, n - 1], u_recv.at[0, n - 1], z * 8 + ty * 2 + c, pb
            )
        )
    for copy in u_copies:
        copy.start()
    va[:, :, at_y] = units[:, y]
    vb[:, :, at_z] = units[z]
    fa_me, fb_me = z * 2 + c, y * 2 + c

    for copy in q_passed:
        copy.wait_recv()
    for n in range(4):
        qa_t[pl.ds(n * 128, 128), :] = qa[n].T
        qb_t[pl.ds(n * 128, 128), :] = qb[n].T

    for copy in u_copies[0::2]:
        copy.wait_recv()
    fb[...] = jnp.dot(vb[...].reshape(128, 512), qb_t[...], preferred_element_type=F32).astype(BF16)

    @pl.loop(1, 8)
    def _(n):
        to = (fb_me + n) % 8
        remote(
            fb.at[pl.ds(pl.multiple_of(to * 16, 16), 16)],
            fb_recv.at[fb_me],
            f_send.at[1],
            f_recv.at[1],
            z * 8 + to,
            pb,
        ).start()

    for copy in u_copies[1::2]:
        copy.wait_recv()
    docs = va[...].reshape(128, 512)
    fa[:, :1024] = jnp.dot(docs, qa_t[...], preferred_element_type=F32).astype(BF16)
    wide = docs.astype(F32)
    square = jnp.broadcast_to(jnp.sum(wide * wide, axis=1, keepdims=True), (128, 128))
    high = square.astype(BF16).astype(F32)
    fa[:, 1024:] = jnp.where(
        lax.broadcasted_iota(jnp.int32, (128, 128), 1) < 64, high, square - high
    ).astype(BF16)

    @pl.loop(1, 8)
    def _(n):
        to = (fa_me + n) % 8
        remote(
            fa.at[pl.ds(pl.multiple_of(to * 16, 16), 16)],
            fa_recv.at[fa_me],
            f_send.at[0],
            f_recv.at[0],
            (to // 2) * 8 + y * 2 + to % 2,
            pb,
        ).start()

    fa_recv[fa_me] = fa[pl.ds(pl.multiple_of(fa_me * 16, 16), 16), :]
    fb_recv[fb_me] = fb[pl.ds(pl.multiple_of(fb_me * 16, 16), 16), :]
    pltpu.make_async_copy(fb_recv.at[pl.ds(0, 7)], fb_recv.at[pl.ds(0, 7)], f_recv.at[1]).wait()
    total_b = fb_recv[0].astype(F32)
    for n in range(1, 8):
        total_b = total_b + fb_recv[n].astype(F32)
    pltpu.make_async_copy(fa_recv.at[pl.ds(0, 7)], fa_recv.at[pl.ds(0, 7)], f_recv.at[0]).wait()
    total_a = fa_recv[0].astype(F32)
    for n in range(1, 8):
        total_a = total_a + fa_recv[n].astype(F32)
    tail = total_a[:, 1024:]
    norm = lax.rsqrt(tail + pltpu.roll(tail, 64, 1) + EPS)[:, 0:1]
    out_ref[:, :1024] = total_a[:, :1024] * norm
    out_ref[:, 1024:] = total_b * norm

    for copy in proj_copies + q_copies + q_passed + u_copies:
        copy.wait_send()
    for g in range(4):
        some = wnd.at[pl.ds(0, 512 if g else 496)]
        pltpu.make_async_copy(some, some, d_send).wait()
    pltpu.make_async_copy(fa.at[pl.ds(0, 112)], fa.at[pl.ds(0, 112)], f_send.at[0]).wait()
    pltpu.make_async_copy(fb.at[pl.ds(0, 112)], fb.at[pl.ds(0, 112)], f_send.at[1]).wait()


def per_device(activations, out_grads, proj_in, proj_out, doc_starts, doc_owner, queries):
    depth_in, depth_out = activations.shape[1], out_grads.shape[1]
    dma = pltpu.SemaphoreType.DMA
    vmem = pltpu.VMEM

    def on_hbm(array):
        return pltpu.with_memory_space_constraint(array, pltpu.HBM)

    return pl.pallas_call(
        kernel,
        out_shape=jax.ShapeDtypeStruct((16, 2048), F32),
        in_specs=[pl.BlockSpec(memory_space=pltpu.HBM)] * 7,
        out_specs=pl.BlockSpec(memory_space=pltpu.VMEM),
        scratch_shapes=[
            vmem((4, SHARE, depth_in), BF16),
            vmem((4, SHARE, depth_out), BF16),
            vmem((64, depth_in), BF16),
            vmem((64, depth_out), BF16),
            vmem((1, 512), jnp.int32),
            vmem((1, 512), jnp.int32),
            vmem((3, SHARE, 128), BF16),
            vmem((SHARE, 128), F32),
            vmem((3, SHARE, 128), BF16),
            vmem((64, SHARE), F32),
            vmem((SLOTS, SHARE), F32),
            vmem((4, 512, 512), BF16),
            vmem((128, 2 * SHARE), BF16),
            vmem((2 * SHARE, 128), BF16),
            vmem((512, 128), BF16),
            vmem((4, 512, 128), BF16),
            vmem((4, 4, 32, 128), BF16),
            vmem((4, 32, 512), BF16),
            vmem((4, 32, 512), BF16),
            vmem((4, 1024, 128), BF16),
            vmem((4, 1024, 128), BF16),
            vmem((512, 1024), BF16),
            vmem((512, 1024), BF16),
            vmem((128, 1152), BF16),
            vmem((128, 1024), BF16),
            vmem((8, 16, 1152), BF16),
            vmem((8, 16, 1024), BF16),
            dma((2, 7)),
            dma((4,)),
            dma((2,)),
            dma((2, 4)),
            dma((2, 4)),
            dma((6,)),
            dma((6,)),
            dma,
            dma((4,)),
            dma((2, 3)),
            dma((2, 3)),
            dma((2,)),
            dma((2,)),
        ],
        compiler_params=pltpu.CompilerParams(
            collective_id=0, has_side_effects=True, vmem_limit_bytes=48 * 1024 * 1024
        ),
    )(
        on_hbm(activations),
        on_hbm(out_grads),
        on_hbm(proj_in.T),
        on_hbm(proj_out.T),
        on_hbm(doc_starts.reshape(1, 512)),
        on_hbm(doc_owner.reshape(1, 512)),
        on_hbm(queries),
    )


def solution(mesh):
    in_specs = (
        P("tok", "pb"),
        P("tok", "pb"),
        P("pb", None),
        P("pb", None),
        P(),
        P(),
        P("pb", "tok"),
    )
    return jax.shard_map(
        per_device, mesh=mesh, in_specs=in_specs, out_specs=P("tok", "pb"), check_vma=False
    )
```

```python
import functools

import jax
import jax.numpy as jnp
from jax import lax
from jax.experimental import pallas as pl
from jax.experimental.pallas import tpu as pltpu
from jax.sharding import PartitionSpec as P

EPS = 1e-06
SHARE = 512
SLOTS = 10
PAIRS = SLOTS // 2
GROUP = 8 * SLOTS
MESH = pl.DeviceIdType.MESH
DEVICES = 128
HALF = 256
NT = (((1,), (1,)), ((), ()))
F32 = jnp.float32
BF16 = jnp.bfloat16


def remote(src, dst, send_sem, recv_sem, tok, pb):
    return pltpu.make_async_remote_copy(
        src_ref=src,
        dst_ref=dst,
        send_sem=send_sem,
        recv_sem=recv_sem,
        device_id=(tok, pb),
        device_id_type=MESH,
    )


def split_slots(numbers):
    quotient = jnp.floor((numbers + 0.5) * (1.0 / SLOTS))
    return quotient, numbers - SLOTS * quotient


def hop_of(t):
    return jnp.where(t == 0, 2, jnp.where(t == 1, 1, jnp.where(t == 2, 3, 0)))


def kernel(
    act_hbm,
    grad_hbm,
    win_hbm,
    wout_hbm,
    starts_hbm,
    owner_hbm,
    q_hbm,
    out_ref,
    act_buf,
    grad_buf,
    win,
    wout,
    starts_ref,
    owner_ref,
    proj_send,
    proj_own,
    proj_recv,
    proj_relay,
    onehot_ref,
    place,
    lhs,
    rhs,
    wnd,
    wnd_recv,
    units,
    va,
    vb,
    qa,
    qb,
    qa_t,
    qb_t,
    fa,
    fb,
    fa_recv,
    fb_recv,
    load_sem,
    w_sem,
    q_sem,
    qs_send,
    qs_recv,
    p_send,
    p_recv,
    d_send,
    d_recv,
    u_send,
    u_recv,
    f_send,
    f_recv,
):
    tok = lax.axis_index("tok")
    pb = lax.axis_index("pb")
    z, y, c = tok // 8, (tok // 2) % 4, tok % 2
    me = tok * 4 + pb

    def loads_of(rows, t, at, sem):
        return [
            pltpu.make_async_copy(grad_hbm.at[rows], grad_buf.at[t, at], load_sem.at[0, sem]),
            pltpu.make_async_copy(act_hbm.at[rows], act_buf.at[t, at], load_sem.at[1, sem]),
        ]

    def half_of(s):
        t = jnp.where(s < 2, 0, 1 + lax.rem(s, 2))
        h = jnp.where((s == 0) | (s == 3) | (s == 4), 0, 1)
        return t, pl.ds(pl.multiple_of(h * HALF, HALF), HALF), h

    def half_loads(s):
        t, at, h = half_of(s)
        start = lax.rem(pb + hop_of(t), 4) * SHARE + h * HALF
        return loads_of(pl.ds(pl.multiple_of(start, HALF), HALF), t, at, s)

    own_loads = loads_of(pl.ds(pl.multiple_of(pb * SHARE, SHARE), SHARE), 3, pl.ds(0, SHARE), 6)
    small = [
        pltpu.make_async_copy(wout_hbm, wout, w_sem.at[0]),
        pltpu.make_async_copy(win_hbm, win, w_sem.at[1]),
        pltpu.make_async_copy(starts_hbm, starts_ref, w_sem.at[2]),
        pltpu.make_async_copy(owner_hbm, owner_ref, w_sem.at[3]),
    ]
    q_loads = [
        pltpu.make_async_copy(q_hbm.at[pl.ds(0, 1024)], qa.at[y], q_sem.at[0]),
        pltpu.make_async_copy(q_hbm.at[pl.ds(1024, 1024)], qb.at[z], q_sem.at[1]),
    ]
    small[0].start()
    small[1].start()
    for copy in half_loads(0) + q_loads:
        copy.start()

    @pl.loop(1, 6)
    def _(s):
        for copy in half_loads(s):
            copy.start()

    for copy in own_loads:
        copy.start()
    small[2].start()
    small[3].start()

    barrier = pltpu.get_barrier_semaphore()

    planes = [lax.rem(pb + n, 4) for n in range(4)]
    for plane in planes[1:]:
        pl.semaphore_signal(barrier, inc=1, device_id=(tok, plane), device_id_type=MESH)

    @pl.loop(1, 32)
    def _(n):
        to = lax.rem(tok + n, 32)
        for plane in planes:
            pl.semaphore_signal(barrier, inc=1, device_id=(to, plane), device_id_type=MESH)

    q_first, q_second, q_passed = [], [], []
    for h, (q_all, place_me) in enumerate(((qa, y), (qb, z))):
        right, left = lax.rem(place_me + 1, 4), lax.rem(place_me + 3, 4)
        for k, (to, row, src, group) in enumerate(
            (
                (right, 0, place_me, q_first),
                (left, 512, place_me, q_first),
                (right, 512, place_me, q_second),
                (left, 0, place_me, q_second),
                (right, 0, left, q_passed),
                (left, 512, right, q_passed),
            )
        ):
            part = q_all.at[src, pl.ds(row, 512)]
            to_tok = z * 8 + to * 2 + c if h == 0 else to * 8 + y * 2 + c
            group.append(remote(part, part, qs_send.at[h, k], qs_recv.at[h, k], to_tok, pb))
    q_copies = q_first + q_second + q_passed

    for copy in small[:2]:
        copy.wait()

    def project(t, at):
        return jnp.concatenate(
            [
                lax.dot_general(act_buf[t, at, :], win[...], NT, preferred_element_type=F32),
                lax.dot_general(grad_buf[t, at, :], wout[...], NT, preferred_element_type=F32),
            ],
            axis=1,
        )

    def relay_copy(s):
        return remote(
            proj_send.at[0, half_of(s)[1]],
            proj_relay.at[s],
            p_send.at[s],
            p_recv.at[s],
            tok,
            lax.rem(pb + 1 + 2 * s, 4),
        )

    def proj_copy(s):
        t, at, _ = half_of(s)
        return remote(
            proj_send.at[t, at], proj_recv.at[t - 1, at], p_send.at[s], p_recv.at[s], tok, lax.rem(pb + hop_of(t), 4)
        )

    @pl.loop(0, 6)
    def _(s):
        for copy in half_loads(s):
            copy.wait()
        t, at, _ = half_of(s)
        both = project(t, at)

        @pl.when(s < 4)
        def _():
            proj_send[t, at, :] = both.astype(BF16)

        @pl.when(s == 0)
        def _():
            pl.semaphore_wait(barrier, DEVICES - 1)
            for copy in q_loads:
                copy.wait()
            for copy in q_first + q_second:
                copy.start()

        @pl.when(s < 2)
        def _():
            relay_copy(s).start()

        @pl.when(s >= 4)
        def _():
            relay_copy(s - 4).wait_recv()
            proj_send[t, at, :] = (both + proj_relay[s - 4].astype(F32)).astype(BF16)

        @pl.when(s >= 2)
        def _():
            proj_copy(s).start()

    for copy in own_loads:
        copy.wait()
    proj_own[...] = project(3, pl.ds(0, SHARE))
    for copy in q_first:
        copy.wait_recv()
    for copy in q_passed:
        copy.start()
    relay_copies = [relay_copy(s) for s in range(2)]
    proj_copies = [proj_copy(s) for s in range(2, 6)]

    for copy in small[2:]:
        copy.wait()
    starts = starts_ref[...]
    begun = starts <= me * SHARE + lax.broadcasted_iota(jnp.int32, (SHARE, 512), 0)
    doc = lax.broadcasted_iota(jnp.int32, (8, 512), 1).astype(F32)
    doc_slot = split_slots(doc)[1]
    slot_before = jnp.where(doc > 0, split_slots(doc - 1)[1], -1.0)
    row_block, row_slot = split_slots(lax.broadcasted_iota(jnp.int32, (GROUP, 128), 0).astype(F32))
    slot_row = row_slot[:, 0:1]
    enters = (doc_slot[0:1, :] == slot_row).astype(F32) - (slot_before[0:1, :] == slot_row).astype(F32)
    onehot_ref[...] = lax.dot_general(
        enters.astype(BF16), begun.astype(F32).astype(BF16), NT, preferred_element_type=F32
    )

    for copy in proj_copies:
        copy.wait_recv()
    proj = proj_own[...]
    for t in range(2):
        proj = proj + proj_recv[t].astype(F32)
    proj = proj.astype(BF16)

    onehot = onehot_ref[...]
    lane = lax.broadcasted_iota(jnp.int32, (GROUP, 128), 1)
    low = lax.broadcasted_iota(jnp.int32, (SHARE, 128), 1) < 64
    wide = proj.astype(F32)
    rhs[...] = jnp.concatenate(
        [jnp.where(low, wide, 0.0), jnp.where(low, 0.0, pltpu.roll(wide, 64, 1))], axis=0
    ).astype(BF16)
    mine = pl.ds(lax.rem(me, 32) * PAIRS, PAIRS)
    far_planes = [planes[2], planes[1], planes[3], planes[0]]

    def send_block(to, plane):
        remote(
            wnd.at[pl.ds(to * PAIRS, PAIRS)],
            wnd_recv.at[z, mine],
            d_send,
            d_recv.at[z],
            to,
            plane,
        ).start()

    @pl.loop(0, 4)
    def _(k):
        g = lax.rem(z + hop_of(k), 4)
        first_r = (64 + g * 16).astype(F32) + 2 * row_block
        for half in range(2):
            pick = (lane.astype(F32) == first_r + half).astype(F32).astype(BF16)
            of_row = lax.dot_general(pick, proj, NT, preferred_element_type=F32)
            lhs[:, pl.ds(half * SHARE, SHARE)] = (onehot * of_row).astype(BF16)
        sums = jnp.dot(lhs[...], rhs[...], preferred_element_type=F32)
        wnd[pl.ds(g * 8 * PAIRS, 8 * PAIRS)] = sums.astype(BF16).reshape(8 * PAIRS, 2, 128)

        @pl.loop(0, 3)
        def _(n):
            row = g * 8 + lax.rem(y + hop_of(n), 4) * 2
            for plane in far_planes:
                send_block(row + c, plane)
                send_block(row + 1 - c, plane)

        for plane in far_planes[:3]:
            send_block(g * 8 + y * 2 + c, plane)
            send_block(g * 8 + y * 2 + 1 - c, plane)
        send_block(g * 8 + y * 2 + 1 - c, pb)

        @pl.when(k < 3)
        def _():
            send_block(g * 8 + y * 2 + c, pb)

    wnd_recv[z, mine] = wnd[pl.ds(tok * PAIRS, PAIRS)]
    lane8 = lax.broadcasted_iota(jnp.int32, (8, 512), 1)
    row8 = lax.broadcasted_iota(jnp.int32, (8, 512), 0)
    first = jnp.broadcast_to(starts, (8, 512)) // SHARE
    last = jnp.where(lane8 == 511, DEVICES - 1, pltpu.roll(first, 511, 1))
    facts = jnp.where(row8 == 0, first.astype(F32), jnp.where(row8 == 1, last.astype(F32), doc_slot))
    rank = owner_ref[...] * 16 + lax.broadcasted_iota(jnp.int32, (1, 512), 1) // 32
    perm = (rank == lax.broadcasted_iota(jnp.int32, (512, 512), 0)).astype(F32).astype(BF16)
    ranked = lax.dot_general(perm, facts.astype(BF16), NT, preferred_element_type=F32)
    block, slot = split_slots(lax.broadcasted_iota(jnp.int32, (8, 32 * SLOTS), 1).astype(F32))
    block = block[0:1, :]
    own_slot = ranked[:, 2:3] == slot[0:1, :]

    @pl.loop(0, 4)
    def _(g):
        from_block = ranked[:, 0:1] - (g * 32).astype(F32)
        to_block = ranked[:, 1:2] - (g * 32).astype(F32)
        inside = (from_block <= block) & (block <= to_block) & own_slot
        place[g] = inside.astype(F32).astype(BF16)

    summed = jnp.zeros((512, 128), F32)
    for n in (2, 3, 1, 0):
        g = (z + n) % 4
        got = wnd_recv.at[g, pl.ds(0, (32 if n else 31) * PAIRS)]
        pltpu.make_async_copy(got, got, d_recv.at[g]).wait()
        summed = summed + jnp.dot(
            place[g], wnd_recv[g].reshape(32 * SLOTS, 128), preferred_element_type=F32
        )
    units[...] = summed.astype(BF16).reshape(4, 4, 32, 128)

    at_y = pl.ds(pl.multiple_of(y * 128, 128), 128)
    at_z = pl.ds(pl.multiple_of(z * 128, 128), 128)
    u_copies = []
    for n in range(1, 4):
        ty, tz = (y + n) % 4, (z + n) % 4
        u_copies.append(
            remote(
                units.at[tz], vb.at[:, :, at_z], u_send.at[1, n - 1], u_recv.at[1, n - 1], tz * 8 + y * 2 + c, pb
            )
        )
        u_copies.append(
            remote(
                units.at[:, ty], va.at[:, :, at_y], u_send.at[0, n - 1], u_recv.at[0, n - 1], z * 8 + ty * 2 + c, pb
            )
        )
    for copy in u_copies:
        copy.start()
    va[:, :, at_y] = units[:, y]
    vb[:, :, at_z] = units[z]
    fa_me, fb_me = z * 2 + c, y * 2 + c

    for copy in q_second + q_passed:
        copy.wait_recv()
    for n in range(4):
        qa_t[pl.ds(n * 128, 128), :] = qa[n].T
        qb_t[pl.ds(n * 128, 128), :] = qb[n].T

    for copy in u_copies[0::2]:
        copy.wait_recv()
    fb[...] = jnp.dot(vb[...].reshape(128, 512), qb_t[...], preferred_element_type=F32).astype(BF16)

    @pl.loop(1, 8)
    def _(n):
        to = (fb_me + n) % 8
        remote(
            fb.at[pl.ds(pl.multiple_of(to * 16, 16), 16)],
            fb_recv.at[fb_me],
            f_send.at[1],
            f_recv.at[1],
            z * 8 + to,
            pb,
        ).start()

    for copy in u_copies[1::2]:
        copy.wait_recv()
    docs = va[...].reshape(128, 512)
    fa[:, :1024] = jnp.dot(docs, qa_t[...], preferred_element_type=F32).astype(BF16)
    wide = docs.astype(F32)
    square = jnp.broadcast_to(jnp.sum(wide * wide, axis=1, keepdims=True), (128, 128))
    high = square.astype(BF16).astype(F32)
    fa[:, 1024:] = jnp.where(
        lax.broadcasted_iota(jnp.int32, (128, 128), 1) < 64, high, square - high
    ).astype(BF16)

    @pl.loop(1, 8)
    def _(n):
        to = (fa_me + n) % 8
        remote(
            fa.at[pl.ds(pl.multiple_of(to * 16, 16), 16)],
            fa_recv.at[fa_me],
            f_send.at[0],
            f_recv.at[0],
            (to // 2) * 8 + y * 2 + to % 2,
            pb,
        ).start()

    fa_recv[fa_me] = fa[pl.ds(pl.multiple_of(fa_me * 16, 16), 16), :]
    fb_recv[fb_me] = fb[pl.ds(pl.multiple_of(fb_me * 16, 16), 16), :]
    pltpu.make_async_copy(fb_recv.at[pl.ds(0, 7)], fb_recv.at[pl.ds(0, 7)], f_recv.at[1]).wait()
    total_b = fb_recv[0].astype(F32)
    for n in range(1, 8):
        total_b = total_b + fb_recv[n].astype(F32)
    pltpu.make_async_copy(fa_recv.at[pl.ds(0, 7)], fa_recv.at[pl.ds(0, 7)], f_recv.at[0]).wait()
    total_a = fa_recv[0].astype(F32)
    for n in range(1, 8):
        total_a = total_a + fa_recv[n].astype(F32)
    tail = total_a[:, 1024:]
    norm = lax.rsqrt(tail + pltpu.roll(tail, 64, 1) + EPS)[:, 0:1]
    out_ref[:, :1024] = total_a[:, :1024] * norm
    out_ref[:, 1024:] = total_b * norm

    for copy in relay_copies + proj_copies + q_copies + u_copies:
        copy.wait_send()
    for g in range(4):
        some = wnd.at[pl.ds(0, (32 if g else 31) * PAIRS)]
        pltpu.make_async_copy(some, some, d_send).wait()
    pltpu.make_async_copy(fa.at[pl.ds(0, 112)], fa.at[pl.ds(0, 112)], f_send.at[0]).wait()
    pltpu.make_async_copy(fb.at[pl.ds(0, 112)], fb.at[pl.ds(0, 112)], f_send.at[1]).wait()


def per_device(activations, out_grads, proj_in, proj_out, doc_starts, doc_owner, queries):
    depth_in, depth_out = activations.shape[1], out_grads.shape[1]
    dma = pltpu.SemaphoreType.DMA
    vmem = pltpu.VMEM

    def on_hbm(array):
        return pltpu.with_memory_space_constraint(array, pltpu.HBM)

    return pl.pallas_call(
        kernel,
        out_shape=jax.ShapeDtypeStruct((16, 2048), F32),
        in_specs=[pl.BlockSpec(memory_space=pltpu.HBM)] * 7,
        out_specs=pl.BlockSpec(memory_space=pltpu.VMEM),
        scratch_shapes=[
            vmem((4, SHARE, depth_in), BF16),
            vmem((4, SHARE, depth_out), BF16),
            vmem((64, depth_in), BF16),
            vmem((64, depth_out), BF16),
            vmem((1, 512), jnp.int32),
            vmem((1, 512), jnp.int32),
            vmem((3, SHARE, 128), BF16),
            vmem((SHARE, 128), F32),
            vmem((2, SHARE, 128), BF16),
            vmem((2, HALF, 128), BF16),
            vmem((GROUP, SHARE), F32),
            vmem((4, 512, 32 * SLOTS), BF16),
            vmem((GROUP, 2 * SHARE), BF16),
            vmem((2 * SHARE, 128), BF16),
            vmem((32 * PAIRS, 2, 128), BF16),
            vmem((4, 32 * PAIRS, 2, 128), BF16),
            vmem((4, 4, 32, 128), BF16),
            vmem((4, 32, 512), BF16),
            vmem((4, 32, 512), BF16),
            vmem((4, 1024, 128), BF16),
            vmem((4, 1024, 128), BF16),
            vmem((512, 1024), BF16),
            vmem((512, 1024), BF16),
            vmem((128, 1152), BF16),
            vmem((128, 1024), BF16),
            vmem((8, 16, 1152), BF16),
            vmem((8, 16, 1024), BF16),
            dma((2, 7)),
            dma((4,)),
            dma((2,)),
            dma((2, 6)),
            dma((2, 6)),
            dma((6,)),
            dma((6,)),
            dma,
            dma((4,)),
            dma((2, 3)),
            dma((2, 3)),
            dma((2,)),
            dma((2,)),
        ],
        compiler_params=pltpu.CompilerParams(
            collective_id=0, has_side_effects=True, vmem_limit_bytes=48 * 1024 * 1024
        ),
    )(
        on_hbm(activations),
        on_hbm(out_grads),
        on_hbm(proj_in.T),
        on_hbm(proj_out.T),
        on_hbm(doc_starts.reshape(1, 512)),
        on_hbm(doc_owner.reshape(1, 512)),
        on_hbm(queries),
    )


def solution(mesh):
    in_specs = (
        P("tok", "pb"),
        P("tok", "pb"),
        P("pb", None),
        P("pb", None),
        P(),
        P(),
        P("pb", "tok"),
    )
    return jax.shard_map(
        per_device, mesh=mesh, in_specs=in_specs, out_specs=P("tok", "pb"), check_vma=False
    )
```

```python
import functools

import jax
import jax.numpy as jnp
from jax import lax
from jax.experimental import pallas as pl
from jax.experimental.pallas import tpu as pltpu
from jax.sharding import PartitionSpec as P

EPS = 1e-06
SHARE = 512
SLOTS = 10
PAIRS = SLOTS // 2
GROUP = 8 * SLOTS
MESH = pl.DeviceIdType.MESH
DEVICES = 128
HALF = 256
NT = (((1,), (1,)), ((), ()))
F32 = jnp.float32
BF16 = jnp.bfloat16


def remote(src, dst, send_sem, recv_sem, tok, pb):
    return pltpu.make_async_remote_copy(
        src_ref=src,
        dst_ref=dst,
        send_sem=send_sem,
        recv_sem=recv_sem,
        device_id=(tok, pb),
        device_id_type=MESH,
    )


def split_slots(numbers):
    quotient = jnp.floor((numbers + 0.5) * (1.0 / SLOTS))
    return quotient, numbers - SLOTS * quotient


def hop_of(t):
    return jnp.where(t == 0, 2, jnp.where(t == 1, 1, jnp.where(t == 2, 3, 0)))


def kernel(
    act_hbm,
    grad_hbm,
    win_hbm,
    wout_hbm,
    starts_hbm,
    owner_hbm,
    q_hbm,
    out_ref,
    act_buf,
    grad_buf,
    win,
    wout,
    starts_ref,
    owner_ref,
    proj_send,
    proj_own,
    proj_recv,
    proj_relay,
    onehot_ref,
    place,
    lhs,
    rhs,
    wnd,
    wnd_recv,
    units,
    va,
    vb,
    qa,
    qb,
    qa_t,
    qb_t,
    fa,
    fb,
    fa_recv,
    fb_recv,
    load_sem,
    w_sem,
    q_sem,
    qs_send,
    qs_recv,
    p_send,
    p_recv,
    d_send,
    d_recv,
    u_send,
    u_recv,
    f_send,
    f_recv,
    round_sem,
):
    tok = lax.axis_index("tok")
    pb = lax.axis_index("pb")
    z, y, c = tok // 8, (tok // 2) % 4, tok % 2
    me = tok * 4 + pb

    def loads_of(rows, t, at, sem):
        return [
            pltpu.make_async_copy(grad_hbm.at[rows], grad_buf.at[t, at], load_sem.at[0, sem]),
            pltpu.make_async_copy(act_hbm.at[rows], act_buf.at[t, at], load_sem.at[1, sem]),
        ]

    def half_of(s):
        t = jnp.where(s < 2, 0, 1 + lax.rem(s, 2))
        h = jnp.where((s == 0) | (s == 3) | (s == 4), 0, 1)
        return t, pl.ds(pl.multiple_of(h * HALF, HALF), HALF), h

    def half_loads(s):
        t, at, h = half_of(s)
        start = lax.rem(pb + hop_of(t), 4) * SHARE + h * HALF
        return loads_of(pl.ds(pl.multiple_of(start, HALF), HALF), t, at, s)

    own_loads = loads_of(pl.ds(pl.multiple_of(pb * SHARE, SHARE), SHARE), 3, pl.ds(0, SHARE), 6)
    small = [
        pltpu.make_async_copy(wout_hbm, wout, w_sem.at[0]),
        pltpu.make_async_copy(win_hbm, win, w_sem.at[1]),
        pltpu.make_async_copy(starts_hbm, starts_ref, w_sem.at[2]),
        pltpu.make_async_copy(owner_hbm, owner_ref, w_sem.at[3]),
    ]
    q_loads = [
        pltpu.make_async_copy(q_hbm.at[pl.ds(0, 1024)], qa.at[y], q_sem.at[0]),
        pltpu.make_async_copy(q_hbm.at[pl.ds(1024, 1024)], qb.at[z], q_sem.at[1]),
    ]
    small[0].start()
    small[1].start()
    for copy in half_loads(0) + q_loads:
        copy.start()

    @pl.loop(1, 6)
    def _(s):
        for copy in half_loads(s):
            copy.start()

    for copy in own_loads:
        copy.start()
    small[2].start()
    small[3].start()

    planes = [lax.rem(pb + n, 4) for n in range(4)]
    on_y = [z * 8 + lax.rem(y + n, 4) * 2 + c for n in range(1, 4)]
    on_z = [lax.rem(z + n, 4) * 8 + y * 2 + c for n in range(1, 4)]
    on_core = [z * 8 + y * 2 + 1 - c]

    def signal(sem, toks):
        for to in toks:
            pl.semaphore_signal(sem, inc=1, device_id=(to, pb), device_id_type=MESH)

    barrier = pltpu.get_barrier_semaphore()
    for plane in planes[1:]:
        pl.semaphore_signal(barrier, inc=1, device_id=(tok, plane), device_id_type=MESH)
    signal(barrier, on_y + on_z + on_core)

    q_first, q_second, q_passed = [], [], []
    for h, (q_all, place_me) in enumerate(((qa, y), (qb, z))):
        right, left = lax.rem(place_me + 1, 4), lax.rem(place_me + 3, 4)
        for k, (to, row, src, group) in enumerate(
            (
                (right, 0, place_me, q_first),
                (left, 512, place_me, q_first),
                (right, 512, place_me, q_second),
                (left, 0, place_me, q_second),
                (right, 0, left, q_passed),
                (left, 512, right, q_passed),
            )
        ):
            part = q_all.at[src, pl.ds(row, 512)]
            to_tok = z * 8 + to * 2 + c if h == 0 else to * 8 + y * 2 + c
            group.append(remote(part, part, qs_send.at[h, k], qs_recv.at[h, k], to_tok, pb))
    q_copies = q_first + q_second + q_passed

    for copy in small[:2]:
        copy.wait()

    def project(t, at):
        return jnp.concatenate(
            [
                lax.dot_general(act_buf[t, at, :], win[...], NT, preferred_element_type=F32),
                lax.dot_general(grad_buf[t, at, :], wout[...], NT, preferred_element_type=F32),
            ],
            axis=1,
        )

    def relay_copy(s):
        return remote(
            proj_send.at[0, half_of(s)[1]],
            proj_relay.at[s],
            p_send.at[s],
            p_recv.at[s],
            tok,
            lax.rem(pb + 1 + 2 * s, 4),
        )

    def proj_copy(s):
        t, at, _ = half_of(s)
        return remote(
            proj_send.at[t, at], proj_recv.at[t - 1, at], p_send.at[s], p_recv.at[s], tok, lax.rem(pb + hop_of(t), 4)
        )

    @pl.loop(0, 6)
    def _(s):
        for copy in half_loads(s):
            copy.wait()
        t, at, _ = half_of(s)
        both = project(t, at)

        @pl.when(s < 4)
        def _():
            proj_send[t, at, :] = both.astype(BF16)

        @pl.when(s == 0)
        def _():
            pl.semaphore_wait(barrier, 10)
            signal(round_sem.at[0], on_y)
            for copy in q_loads:
                copy.wait()
            for copy in q_first + q_second:
                copy.start()

        @pl.when(s < 2)
        def _():
            relay_copy(s).start()

        @pl.when(s == 2)
        def _():
            pl.semaphore_wait(round_sem.at[0], 3)
            signal(round_sem.at[1], on_z)

        @pl.when(s == 4)
        def _():
            pl.semaphore_wait(round_sem.at[1], 3)
            signal(round_sem.at[2], on_core)

        @pl.when(s >= 4)
        def _():
            relay_copy(s - 4).wait_recv()
            proj_send[t, at, :] = (both + proj_relay[s - 4].astype(F32)).astype(BF16)

        @pl.when(s >= 2)
        def _():
            proj_copy(s).start()

    for copy in own_loads:
        copy.wait()
    proj_own[...] = project(3, pl.ds(0, SHARE))
    pl.semaphore_wait(round_sem.at[2], 1)
    for copy in q_first:
        copy.wait_recv()
    for copy in q_passed:
        copy.start()
    relay_copies = [relay_copy(s) for s in range(2)]
    proj_copies = [proj_copy(s) for s in range(2, 6)]

    for copy in small[2:]:
        copy.wait()
    starts = starts_ref[...]
    begun = starts <= me * SHARE + lax.broadcasted_iota(jnp.int32, (SHARE, 512), 0)
    doc = lax.broadcasted_iota(jnp.int32, (8, 512), 1).astype(F32)
    doc_slot = split_slots(doc)[1]
    slot_before = jnp.where(doc > 0, split_slots(doc - 1)[1], -1.0)
    row_block, row_slot = split_slots(lax.broadcasted_iota(jnp.int32, (GROUP, 128), 0).astype(F32))
    slot_row = row_slot[:, 0:1]
    enters = (doc_slot[0:1, :] == slot_row).astype(F32) - (slot_before[0:1, :] == slot_row).astype(F32)
    onehot_ref[...] = lax.dot_general(
        enters.astype(BF16), begun.astype(F32).astype(BF16), NT, preferred_element_type=F32
    )

    for copy in proj_copies:
        copy.wait_recv()
    proj = proj_own[...]
    for t in range(2):
        proj = proj + proj_recv[t].astype(F32)
    proj = proj.astype(BF16)

    onehot = onehot_ref[...]
    lane = lax.broadcasted_iota(jnp.int32, (GROUP, 128), 1)
    low = lax.broadcasted_iota(jnp.int32, (SHARE, 128), 1) < 64
    wide = proj.astype(F32)
    rhs[...] = jnp.concatenate(
        [jnp.where(low, wide, 0.0), jnp.where(low, 0.0, pltpu.roll(wide, 64, 1))], axis=0
    ).astype(BF16)
    mine = pl.ds(lax.rem(me, 32) * PAIRS, PAIRS)
    far_planes = [planes[2], planes[1], planes[3], planes[0]]

    def send_block(to, plane):
        remote(
            wnd.at[pl.ds(to * PAIRS, PAIRS)],
            wnd_recv.at[z, mine],
            d_send,
            d_recv.at[z],
            to,
            plane,
        ).start()

    @pl.loop(0, 4)
    def _(k):
        g = lax.rem(z + hop_of(k), 4)
        first_r = (64 + g * 16).astype(F32) + 2 * row_block
        for half in range(2):
            pick = (lane.astype(F32) == first_r + half).astype(F32).astype(BF16)
            of_row = lax.dot_general(pick, proj, NT, preferred_element_type=F32)
            lhs[:, pl.ds(half * SHARE, SHARE)] = (onehot * of_row).astype(BF16)
        sums = jnp.dot(lhs[...], rhs[...], preferred_element_type=F32)
        wnd[pl.ds(g * 8 * PAIRS, 8 * PAIRS)] = sums.astype(BF16).reshape(8 * PAIRS, 2, 128)

        @pl.loop(0, 3)
        def _(n):
            row = g * 8 + lax.rem(y + hop_of(n), 4) * 2
            for plane in far_planes:
                send_block(row + c, plane)
                send_block(row + 1 - c, plane)

        for plane in far_planes[:3]:
            send_block(g * 8 + y * 2 + c, plane)
            send_block(g * 8 + y * 2 + 1 - c, plane)
        send_block(g * 8 + y * 2 + 1 - c, pb)

        @pl.when(k < 3)
        def _():
            send_block(g * 8 + y * 2 + c, pb)

    wnd_recv[z, mine] = wnd[pl.ds(tok * PAIRS, PAIRS)]
    lane8 = lax.broadcasted_iota(jnp.int32, (8, 512), 1)
    row8 = lax.broadcasted_iota(jnp.int32, (8, 512), 0)
    first = jnp.broadcast_to(starts, (8, 512)) // SHARE
    last = jnp.where(lane8 == 511, DEVICES - 1, pltpu.roll(first, 511, 1))
    facts = jnp.where(row8 == 0, first.astype(F32), jnp.where(row8 == 1, last.astype(F32), doc_slot))
    rank = owner_ref[...] * 16 + lax.broadcasted_iota(jnp.int32, (1, 512), 1) // 32
    perm = (rank == lax.broadcasted_iota(jnp.int32, (512, 512), 0)).astype(F32).astype(BF16)
    ranked = lax.dot_general(perm, facts.astype(BF16), NT, preferred_element_type=F32)
    block, slot = split_slots(lax.broadcasted_iota(jnp.int32, (8, 32 * SLOTS), 1).astype(F32))
    block = block[0:1, :]
    own_slot = ranked[:, 2:3] == slot[0:1, :]

    @pl.loop(0, 4)
    def _(g):
        from_block = ranked[:, 0:1] - (g * 32).astype(F32)
        to_block = ranked[:, 1:2] - (g * 32).astype(F32)
        inside = (from_block <= block) & (block <= to_block) & own_slot
        place[g] = inside.astype(F32).astype(BF16)

    summed = jnp.zeros((512, 128), F32)
    for n in (2, 3, 1, 0):
        g = (z + n) % 4
        got = wnd_recv.at[g, pl.ds(0, (32 if n else 31) * PAIRS)]
        pltpu.make_async_copy(got, got, d_recv.at[g]).wait()
        summed = summed + jnp.dot(
            place[g], wnd_recv[g].reshape(32 * SLOTS, 128), preferred_element_type=F32
        )
    units[...] = summed.astype(BF16).reshape(4, 4, 32, 128)

    at_y = pl.ds(pl.multiple_of(y * 128, 128), 128)
    at_z = pl.ds(pl.multiple_of(z * 128, 128), 128)
    u_copies = []
    for n in range(1, 4):
        ty, tz = (y + n) % 4, (z + n) % 4
        u_copies.append(
            remote(
                units.at[tz], vb.at[:, :, at_z], u_send.at[1, n - 1], u_recv.at[1, n - 1], tz * 8 + y * 2 + c, pb
            )
        )
        u_copies.append(
            remote(
                units.at[:, ty], va.at[:, :, at_y], u_send.at[0, n - 1], u_recv.at[0, n - 1], z * 8 + ty * 2 + c, pb
            )
        )
    for copy in u_copies:
        copy.start()
    va[:, :, at_y] = units[:, y]
    vb[:, :, at_z] = units[z]
    fa_me, fb_me = z * 2 + c, y * 2 + c

    for copy in q_second + q_passed:
        copy.wait_recv()
    for n in range(4):
        qa_t[pl.ds(n * 128, 128), :] = qa[n].T
        qb_t[pl.ds(n * 128, 128), :] = qb[n].T

    for copy in u_copies[0::2]:
        copy.wait_recv()
    fb[...] = jnp.dot(vb[...].reshape(128, 512), qb_t[...], preferred_element_type=F32).astype(BF16)

    @pl.loop(1, 8)
    def _(n):
        to = (fb_me + n) % 8
        remote(
            fb.at[pl.ds(pl.multiple_of(to * 16, 16), 16)],
            fb_recv.at[fb_me],
            f_send.at[1],
            f_recv.at[1],
            z * 8 + to,
            pb,
        ).start()

    for copy in u_copies[1::2]:
        copy.wait_recv()
    docs = va[...].reshape(128, 512)
    fa[:, :1024] = jnp.dot(docs, qa_t[...], preferred_element_type=F32).astype(BF16)
    wide = docs.astype(F32)
    square = jnp.broadcast_to(jnp.sum(wide * wide, axis=1, keepdims=True), (128, 128))
    high = square.astype(BF16).astype(F32)
    fa[:, 1024:] = jnp.where(
        lax.broadcasted_iota(jnp.int32, (128, 128), 1) < 64, high, square - high
    ).astype(BF16)

    @pl.loop(1, 8)
    def _(n):
        to = (fa_me + n) % 8
        remote(
            fa.at[pl.ds(pl.multiple_of(to * 16, 16), 16)],
            fa_recv.at[fa_me],
            f_send.at[0],
            f_recv.at[0],
            (to // 2) * 8 + y * 2 + to % 2,
            pb,
        ).start()

    fa_recv[fa_me] = fa[pl.ds(pl.multiple_of(fa_me * 16, 16), 16), :]
    fb_recv[fb_me] = fb[pl.ds(pl.multiple_of(fb_me * 16, 16), 16), :]
    pltpu.make_async_copy(fb_recv.at[pl.ds(0, 7)], fb_recv.at[pl.ds(0, 7)], f_recv.at[1]).wait()
    total_b = fb_recv[0].astype(F32)
    for n in range(1, 8):
        total_b = total_b + fb_recv[n].astype(F32)
    pltpu.make_async_copy(fa_recv.at[pl.ds(0, 7)], fa_recv.at[pl.ds(0, 7)], f_recv.at[0]).wait()
    total_a = fa_recv[0].astype(F32)
    for n in range(1, 8):
        total_a = total_a + fa_recv[n].astype(F32)
    tail = total_a[:, 1024:]
    norm = lax.rsqrt(tail + pltpu.roll(tail, 64, 1) + EPS)[:, 0:1]
    out_ref[:, :1024] = total_a[:, :1024] * norm
    out_ref[:, 1024:] = total_b * norm

    for copy in relay_copies + proj_copies + q_copies + u_copies:
        copy.wait_send()
    for g in range(4):
        some = wnd.at[pl.ds(0, (32 if g else 31) * PAIRS)]
        pltpu.make_async_copy(some, some, d_send).wait()
    pltpu.make_async_copy(fa.at[pl.ds(0, 112)], fa.at[pl.ds(0, 112)], f_send.at[0]).wait()
    pltpu.make_async_copy(fb.at[pl.ds(0, 112)], fb.at[pl.ds(0, 112)], f_send.at[1]).wait()


def per_device(activations, out_grads, proj_in, proj_out, doc_starts, doc_owner, queries):
    depth_in, depth_out = activations.shape[1], out_grads.shape[1]
    dma = pltpu.SemaphoreType.DMA
    vmem = pltpu.VMEM

    def on_hbm(array):
        return pltpu.with_memory_space_constraint(array, pltpu.HBM)

    return pl.pallas_call(
        kernel,
        out_shape=jax.ShapeDtypeStruct((16, 2048), F32),
        in_specs=[pl.BlockSpec(memory_space=pltpu.HBM)] * 7,
        out_specs=pl.BlockSpec(memory_space=pltpu.VMEM),
        scratch_shapes=[
            vmem((4, SHARE, depth_in), BF16),
            vmem((4, SHARE, depth_out), BF16),
            vmem((64, depth_in), BF16),
            vmem((64, depth_out), BF16),
            vmem((1, 512), jnp.int32),
            vmem((1, 512), jnp.int32),
            vmem((3, SHARE, 128), BF16),
            vmem((SHARE, 128), F32),
            vmem((2, SHARE, 128), BF16),
            vmem((2, HALF, 128), BF16),
            vmem((GROUP, SHARE), F32),
            vmem((4, 512, 32 * SLOTS), BF16),
            vmem((GROUP, 2 * SHARE), BF16),
            vmem((2 * SHARE, 128), BF16),
            vmem((32 * PAIRS, 2, 128), BF16),
            vmem((4, 32 * PAIRS, 2, 128), BF16),
            vmem((4, 4, 32, 128), BF16),
            vmem((4, 32, 512), BF16),
            vmem((4, 32, 512), BF16),
            vmem((4, 1024, 128), BF16),
            vmem((4, 1024, 128), BF16),
            vmem((512, 1024), BF16),
            vmem((512, 1024), BF16),
            vmem((128, 1152), BF16),
            vmem((128, 1024), BF16),
            vmem((8, 16, 1152), BF16),
            vmem((8, 16, 1024), BF16),
            dma((2, 7)),
            dma((4,)),
            dma((2,)),
            dma((2, 6)),
            dma((2, 6)),
            dma((6,)),
            dma((6,)),
            dma,
            dma((4,)),
            dma((2, 3)),
            dma((2, 3)),
            dma((2,)),
            dma((2,)),
            pltpu.SemaphoreType.REGULAR((3,)),
        ],
        compiler_params=pltpu.CompilerParams(
            collective_id=0, has_side_effects=True, vmem_limit_bytes=48 * 1024 * 1024
        ),
    )(
        on_hbm(activations),
        on_hbm(out_grads),
        on_hbm(proj_in.T),
        on_hbm(proj_out.T),
        on_hbm(doc_starts.reshape(1, 512)),
        on_hbm(doc_owner.reshape(1, 512)),
        on_hbm(queries),
    )


def solution(mesh):
    in_specs = (
        P("tok", "pb"),
        P("tok", "pb"),
        P("pb", None),
        P("pb", None),
        P(),
        P(),
        P("pb", "tok"),
    )
    return jax.shard_map(
        per_device, mesh=mesh, in_specs=in_specs, out_specs=P("tok", "pb"), check_vma=False
    )
```

```python
import functools

import jax
import jax.numpy as jnp
from jax import lax
from jax.experimental import pallas as pl
from jax.experimental.pallas import tpu as pltpu
from jax.sharding import PartitionSpec as P

EPS = 1e-06
SHARE = 512
SLOTS = 10
PAIRS = SLOTS // 2
GROUP = 8 * SLOTS
MESH = pl.DeviceIdType.MESH
DEVICES = 128
HALF = 256
NT = (((1,), (1,)), ((), ()))
F32 = jnp.float32
BF16 = jnp.bfloat16


def remote(src, dst, send_sem, recv_sem, tok, pb):
    return pltpu.make_async_remote_copy(
        src_ref=src,
        dst_ref=dst,
        send_sem=send_sem,
        recv_sem=recv_sem,
        device_id=(tok, pb),
        device_id_type=MESH,
    )


def drain(ref, sem):
    pltpu.make_async_copy(ref, ref, sem).wait()


def split_slots(numbers):
    quotient = jnp.floor((numbers + 0.5) * (1.0 / SLOTS))
    return quotient, numbers - SLOTS * quotient


def hop_of(t):
    return jnp.where(t == 0, 2, jnp.where(t == 1, 1, jnp.where(t == 2, 3, 0)))


def kernel(
    act_hbm,
    grad_hbm,
    win_hbm,
    wout_hbm,
    starts_hbm,
    owner_hbm,
    q_hbm,
    out_ref,
    tokens,
    weights,
    docs_ref,
    proj_send,
    proj_own,
    proj_recv,
    proj_relay,
    onehot_ref,
    place,
    lhs,
    rhs,
    wnd,
    wnd_recv,
    units,
    va,
    vb,
    q_all,
    qa_t,
    qb_t,
    fa,
    fb,
    fa_recv,
    fb_recv,
    load_sem,
    w_sem,
    docs_sem,
    q_sem,
    qs_send,
    qs_recv,
    p_send,
    relay_recv,
    p_recv,
    d_send,
    d_recv,
    u_send,
    u_recv,
    f_send,
    f_recv,
    round_sem,
):
    tok = lax.axis_index("tok")
    pb = lax.axis_index("pb")
    z, y, c = tok // 8, (tok // 2) % 4, tok % 2
    me = tok * 4 + pb

    depth_in = act_hbm.shape[1]
    depth_out = grad_hbm.shape[1]
    of_act, of_grad = pl.ds(0, depth_in), pl.ds(depth_in, depth_out)

    def loads_of(rows, t, at, sem):
        return [
            pltpu.make_async_copy(grad_hbm.at[rows], tokens.at[t, at, of_grad], load_sem.at[sem]),
            pltpu.make_async_copy(act_hbm.at[rows], tokens.at[t, at, of_act], load_sem.at[sem]),
        ]

    def half_of(s):
        t = jnp.where(s < 2, 0, 1 + lax.rem(s, 2))
        h = jnp.where((s == 0) | (s == 3) | (s == 4), 0, 1)
        return t, pl.ds(pl.multiple_of(h * HALF, HALF), HALF), h

    def half_loads(s):
        t, at, h = half_of(s)
        start = lax.rem(pb + hop_of(t), 4) * SHARE + h * HALF
        return loads_of(pl.ds(pl.multiple_of(start, HALF), HALF), t, at, s)

    own_loads = loads_of(pl.ds(pl.multiple_of(pb * SHARE, SHARE), SHARE), 3, pl.ds(0, SHARE), 6)
    small = [
        pltpu.make_async_copy(wout_hbm, weights.at[pl.ds(64, 64), of_grad], w_sem),
        pltpu.make_async_copy(win_hbm, weights.at[pl.ds(0, 64), of_act], w_sem),
        pltpu.make_async_copy(starts_hbm, docs_ref.at[0], docs_sem),
        pltpu.make_async_copy(owner_hbm, docs_ref.at[1], docs_sem),
    ]
    q_loads = [
        pltpu.make_async_copy(q_hbm.at[pl.ds(0, 1024)], q_all.at[0, y], q_sem),
        pltpu.make_async_copy(q_hbm.at[pl.ds(1024, 1024)], q_all.at[1, z], q_sem),
    ]
    small[0].start()
    small[1].start()
    for copy in half_loads(0) + q_loads:
        copy.start()

    @pl.loop(1, 6)
    def _(s):
        for copy in half_loads(s):
            copy.start()

    for copy in own_loads:
        copy.start()
    small[2].start()
    small[3].start()

    planes = [lax.rem(pb + n, 4) for n in range(4)]
    on_y = [z * 8 + lax.rem(y + n, 4) * 2 + c for n in range(1, 4)]
    on_z = [lax.rem(z + n, 4) * 8 + y * 2 + c for n in range(1, 4)]
    on_core = [z * 8 + y * 2 + 1 - c]

    def signal(sem, toks):
        for to in toks:
            pl.semaphore_signal(sem, inc=1, device_id=(to, pb), device_id_type=MESH)

    barrier = pltpu.get_barrier_semaphore()
    for plane in planes[1:]:
        pl.semaphore_signal(barrier, inc=1, device_id=(tok, plane), device_id_type=MESH)
    signal(barrier, on_y + on_z + on_core)

    q_first, q_second, q_passed = [], [], []
    for h, place_me in enumerate((y, z)):
        right, left = lax.rem(place_me + 1, 4), lax.rem(place_me + 3, 4)
        for k, (to, row, src, group) in enumerate(
            (
                (right, 0, place_me, q_first),
                (left, 512, place_me, q_first),
                (right, 512, place_me, q_second),
                (left, 0, place_me, q_second),
                (right, 0, left, q_passed),
                (left, 512, right, q_passed),
            )
        ):
            part = q_all.at[h, src, pl.ds(row, 512)]
            to_tok = z * 8 + to * 2 + c if h == 0 else to * 8 + y * 2 + c
            group.append(remote(part, part, qs_send, qs_recv.at[0 if k < 2 else 1], to_tok, pb))

    weights[:64, depth_in:] = jnp.zeros((64, depth_out), BF16)
    weights[64:, :depth_in] = jnp.zeros((64, depth_in), BF16)
    drain(weights.at[pl.ds(0, 64)], w_sem)

    def project(t, at):
        return lax.dot_general(tokens[t, at, :], weights[...], NT, preferred_element_type=F32)

    def relay_copy(s):
        return remote(
            proj_send.at[0, half_of(s)[1]],
            proj_relay.at[s],
            p_send,
            relay_recv.at[s],
            tok,
            lax.rem(pb + 1 + 2 * s, 4),
        )

    def proj_copy(s):
        t, at, _ = half_of(s)
        return remote(
            proj_send.at[t, at], proj_recv.at[t - 1, at], p_send, p_recv, tok, lax.rem(pb + hop_of(t), 4)
        )

    @pl.loop(0, 6)
    def _(s):
        t, at, _ = half_of(s)
        drain(tokens.at[t, at], load_sem.at[s])
        both = project(t, at)

        @pl.when(s < 4)
        def _():
            proj_send[t, at, :] = both.astype(BF16)

        @pl.when(s == 0)
        def _():
            pl.semaphore_wait(barrier, 10)
            signal(round_sem.at[0], on_y)

        @pl.when(s < 2)
        def _():
            relay_copy(s).start()

        @pl.when(s == 2)
        def _():
            pl.semaphore_wait(round_sem.at[0], 3)
            signal(round_sem.at[1], on_z)

        @pl.when(s == 4)
        def _():
            pl.semaphore_wait(round_sem.at[1], 3)
            signal(round_sem.at[2], on_core)

        @pl.when(s >= 4)
        def _():
            drain(proj_relay.at[s - 4], relay_recv.at[s - 4])
            proj_send[t, at, :] = (both + proj_relay[s - 4].astype(F32)).astype(BF16)

        @pl.when(s >= 2)
        def _():
            proj_copy(s).start()

        @pl.when(s == 0)
        def _():
            drain(q_all.at[0, pl.ds(0, 2)], q_sem)
            for copy in q_first:
                copy.start()

        @pl.when(s == 0)
        def _():
            for copy in q_second:
                copy.start()

    drain(tokens.at[3], load_sem.at[6])
    proj_own[...] = project(3, pl.ds(0, SHARE))
    pl.semaphore_wait(round_sem.at[2], 1)
    drain(q_all.at[0, pl.ds(0, 2)], qs_recv.at[0])
    for copy in q_passed:
        copy.start()

    drain(docs_ref, docs_sem)
    starts = docs_ref[0]
    begun = starts <= me * SHARE + lax.broadcasted_iota(jnp.int32, (SHARE, 512), 0)
    doc = lax.broadcasted_iota(jnp.int32, (8, 512), 1).astype(F32)
    doc_slot = split_slots(doc)[1]
    slot_before = jnp.where(doc > 0, split_slots(doc - 1)[1], -1.0)
    row_block, row_slot = split_slots(lax.broadcasted_iota(jnp.int32, (GROUP, 128), 0).astype(F32))
    slot_row = row_slot[:, 0:1]
    enters = (doc_slot[0:1, :] == slot_row).astype(F32) - (slot_before[0:1, :] == slot_row).astype(F32)
    onehot_ref[...] = lax.dot_general(
        enters.astype(BF16), begun.astype(F32).astype(BF16), NT, preferred_element_type=F32
    )

    drain(proj_recv, p_recv)
    proj = proj_own[...]
    for t in range(2):
        proj = proj + proj_recv[t].astype(F32)
    proj = proj.astype(BF16)

    onehot = onehot_ref[...]
    lane = lax.broadcasted_iota(jnp.int32, (GROUP, 128), 1)
    low = lax.broadcasted_iota(jnp.int32, (SHARE, 128), 1) < 64
    wide = proj.astype(F32)
    rhs[...] = jnp.concatenate(
        [jnp.where(low, wide, 0.0), jnp.where(low, 0.0, pltpu.roll(wide, 64, 1))], axis=0
    ).astype(BF16)
    mine = pl.ds(lax.rem(me, 32) * PAIRS, PAIRS)
    far_planes = [planes[2], planes[1], planes[3], planes[0]]

    def send_block(to, plane):
        remote(
            wnd.at[pl.ds(to * PAIRS, PAIRS)],
            wnd_recv.at[z, mine],
            d_send,
            d_recv.at[z],
            to,
            plane,
        ).start()

    @pl.loop(0, 4)
    def _(k):
        g = lax.rem(z + hop_of(k), 4)
        first_r = (64 + g * 16).astype(F32) + 2 * row_block
        for half in range(2):
            pick = (lane.astype(F32) == first_r + half).astype(F32).astype(BF16)
            of_row = lax.dot_general(pick, proj, NT, preferred_element_type=F32)
            lhs[:, pl.ds(half * SHARE, SHARE)] = (onehot * of_row).astype(BF16)
        sums = jnp.dot(lhs[...], rhs[...], preferred_element_type=F32)
        wnd[pl.ds(g * 8 * PAIRS, 8 * PAIRS)] = sums.astype(BF16).reshape(8 * PAIRS, 2, 128)

        @pl.loop(0, 3)
        def _(n):
            row = g * 8 + lax.rem(y + hop_of(n), 4) * 2
            for plane in far_planes:
                send_block(row + c, plane)
                send_block(row + 1 - c, plane)

        for plane in far_planes[:3]:
            send_block(g * 8 + y * 2 + c, plane)
            send_block(g * 8 + y * 2 + 1 - c, plane)
        send_block(g * 8 + y * 2 + 1 - c, pb)

        @pl.when(k < 3)
        def _():
            send_block(g * 8 + y * 2 + c, pb)

    wnd_recv[z, mine] = wnd[pl.ds(tok * PAIRS, PAIRS)]
    lane8 = lax.broadcasted_iota(jnp.int32, (8, 512), 1)
    row8 = lax.broadcasted_iota(jnp.int32, (8, 512), 0)
    first = jnp.broadcast_to(starts, (8, 512)) // SHARE
    last = jnp.where(lane8 == 511, DEVICES - 1, pltpu.roll(first, 511, 1))
    facts = jnp.where(row8 == 0, first.astype(F32), jnp.where(row8 == 1, last.astype(F32), doc_slot))
    rank = docs_ref[1] * 16 + lax.broadcasted_iota(jnp.int32, (1, 512), 1) // 32
    perm = (rank == lax.broadcasted_iota(jnp.int32, (512, 512), 0)).astype(F32).astype(BF16)
    ranked = lax.dot_general(perm, facts.astype(BF16), NT, preferred_element_type=F32)
    block, slot = split_slots(lax.broadcasted_iota(jnp.int32, (8, 32 * SLOTS), 1).astype(F32))
    block = block[0:1, :]
    own_slot = ranked[:, 2:3] == slot[0:1, :]

    @pl.loop(0, 4)
    def _(g):
        from_block = ranked[:, 0:1] - (g * 32).astype(F32)
        to_block = ranked[:, 1:2] - (g * 32).astype(F32)
        inside = (from_block <= block) & (block <= to_block) & own_slot
        place[g] = inside.astype(F32).astype(BF16)

    summed = jnp.zeros((512, 128), F32)
    for n in (2, 3, 1, 0):
        g = (z + n) % 4
        got = wnd_recv.at[g, pl.ds(0, (32 if n else 31) * PAIRS)]
        drain(got, d_recv.at[g])
        summed = summed + jnp.dot(
            place[g], wnd_recv[g].reshape(32 * SLOTS, 128), preferred_element_type=F32
        )
    units[...] = summed.astype(BF16).reshape(4, 4, 32, 128)

    at_y = pl.ds(pl.multiple_of(y * 128, 128), 128)
    at_z = pl.ds(pl.multiple_of(z * 128, 128), 128)
    u_copies = []
    for n in range(1, 4):
        ty, tz = (y + n) % 4, (z + n) % 4
        u_copies.append(
            remote(
                units.at[tz], vb.at[:, :, at_z], u_send, u_recv.at[1], tz * 8 + y * 2 + c, pb
            )
        )
        u_copies.append(
            remote(
                units.at[:, ty], va.at[:, :, at_y], u_send, u_recv.at[0], z * 8 + ty * 2 + c, pb
            )
        )
    for copy in u_copies:
        copy.start()
    va[:, :, at_y] = units[:, y]
    vb[:, :, at_z] = units[z]
    fa_me, fb_me = z * 2 + c, y * 2 + c

    drain(q_all.at[0], qs_recv.at[1])
    for n in range(4):
        qa_t[pl.ds(n * 128, 128), :] = q_all[0, n].T
        qb_t[pl.ds(n * 128, 128), :] = q_all[1, n].T

    drain(vb.at[:, :, pl.ds(0, 384)], u_recv.at[1])
    fb[...] = jnp.dot(vb[...].reshape(128, 512), qb_t[...], preferred_element_type=F32).astype(BF16)

    @pl.loop(1, 8)
    def _(n):
        to = (fb_me + n) % 8
        remote(
            fb.at[pl.ds(pl.multiple_of(to * 16, 16), 16)],
            fb_recv.at[fb_me],
            f_send,
            f_recv.at[1],
            z * 8 + to,
            pb,
        ).start()

    drain(va.at[:, :, pl.ds(0, 384)], u_recv.at[0])
    docs = va[...].reshape(128, 512)
    fa[:, :1024] = jnp.dot(docs, qa_t[...], preferred_element_type=F32).astype(BF16)
    wide = docs.astype(F32)
    square = jnp.broadcast_to(jnp.sum(wide * wide, axis=1, keepdims=True), (128, 128))
    high = square.astype(BF16).astype(F32)
    fa[:, 1024:] = jnp.where(
        lax.broadcasted_iota(jnp.int32, (128, 128), 1) < 64, high, square - high
    ).astype(BF16)

    @pl.loop(1, 8)
    def _(n):
        to = (fa_me + n) % 8
        remote(
            fa.at[pl.ds(pl.multiple_of(to * 16, 16), 16)],
            fa_recv.at[fa_me],
            f_send,
            f_recv.at[0],
            (to // 2) * 8 + y * 2 + to % 2,
            pb,
        ).start()

    fa_recv[fa_me] = fa[pl.ds(pl.multiple_of(fa_me * 16, 16), 16), :]
    fb_recv[fb_me] = fb[pl.ds(pl.multiple_of(fb_me * 16, 16), 16), :]
    drain(fb_recv.at[pl.ds(0, 7)], f_recv.at[1])
    total_b = fb_recv[0].astype(F32)
    for n in range(1, 8):
        total_b = total_b + fb_recv[n].astype(F32)
    drain(fa_recv.at[pl.ds(0, 7)], f_recv.at[0])
    total_a = fa_recv[0].astype(F32)
    for n in range(1, 8):
        total_a = total_a + fa_recv[n].astype(F32)
    tail = total_a[:, 1024:]
    norm = lax.rsqrt(tail + pltpu.roll(tail, 64, 1) + EPS)[:, 0:1]
    out_ref[:, :1024] = total_a[:, :1024] * norm
    out_ref[:, 1024:] = total_b * norm

    drain(proj_send, p_send)
    drain(q_all.at[:, pl.ds(0, 3)], qs_send)
    for n in range(2):
        drain(va.at[:, :, pl.ds(0, 384)], u_send)
    for g in range(4):
        drain(wnd.at[pl.ds(0, (32 if g else 31) * PAIRS)], d_send)
    drain(fa.at[pl.ds(0, 112)], f_send)
    drain(fb.at[pl.ds(0, 112)], f_send)


def per_device(activations, out_grads, proj_in, proj_out, doc_starts, doc_owner, queries):
    depth_in, depth_out = activations.shape[1], out_grads.shape[1]
    dma = pltpu.SemaphoreType.DMA
    vmem = pltpu.VMEM

    def on_hbm(array):
        return pltpu.with_memory_space_constraint(array, pltpu.HBM)

    return pl.pallas_call(
        kernel,
        out_shape=jax.ShapeDtypeStruct((16, 2048), F32),
        in_specs=[pl.BlockSpec(memory_space=pltpu.HBM)] * 7,
        out_specs=pl.BlockSpec(memory_space=pltpu.VMEM),
        scratch_shapes=[
            vmem((4, SHARE, depth_in + depth_out), BF16),
            vmem((128, depth_in + depth_out), BF16),
            vmem((2, 1, 512), jnp.int32),
            vmem((3, SHARE, 128), BF16),
            vmem((SHARE, 128), F32),
            vmem((2, SHARE, 128), BF16),
            vmem((2, HALF, 128), BF16),
            vmem((GROUP, SHARE), F32),
            vmem((4, 512, 32 * SLOTS), BF16),
            vmem((GROUP, 2 * SHARE), BF16),
            vmem((2 * SHARE, 128), BF16),
            vmem((32 * PAIRS, 2, 128), BF16),
            vmem((4, 32 * PAIRS, 2, 128), BF16),
            vmem((4, 4, 32, 128), BF16),
            vmem((4, 32, 512), BF16),
            vmem((4, 32, 512), BF16),
            vmem((2, 4, 1024, 128), BF16),
            vmem((512, 1024), BF16),
            vmem((512, 1024), BF16),
            vmem((128, 1152), BF16),
            vmem((128, 1024), BF16),
            vmem((8, 16, 1152), BF16),
            vmem((8, 16, 1024), BF16),
            dma((7,)),
            dma,
            dma,
            dma,
            dma,
            dma((2,)),
            dma,
            dma((2,)),
            dma,
            dma,
            dma((4,)),
            dma,
            dma((2,)),
            dma,
            dma((2,)),
            pltpu.SemaphoreType.REGULAR((3,)),
        ],
        compiler_params=pltpu.CompilerParams(
            collective_id=0, has_side_effects=True, vmem_limit_bytes=48 * 1024 * 1024
        ),
    )(
        on_hbm(activations),
        on_hbm(out_grads),
        on_hbm(proj_in.T),
        on_hbm(proj_out.T),
        on_hbm(doc_starts.reshape(1, 512)),
        on_hbm(doc_owner.reshape(1, 512)),
        on_hbm(queries),
    )


def solution(mesh):
    in_specs = (
        P("tok", "pb"),
        P("tok", "pb"),
        P("pb", None),
        P("pb", None),
        P(),
        P(),
        P("pb", "tok"),
    )
    return jax.shard_map(
        per_device, mesh=mesh, in_specs=in_specs, out_specs=P("tok", "pb"), check_vma=False
    )
```

```python
import functools

import jax
import jax.numpy as jnp
from jax import lax
from jax.experimental import pallas as pl
from jax.experimental.pallas import tpu as pltpu
from jax.sharding import PartitionSpec as P

EPS = 1e-06
SHARE = 512
SLOTS = 10
PAIRS = SLOTS // 2
GROUP = 8 * SLOTS
MESH = pl.DeviceIdType.MESH
DEVICES = 128
HALF = 256
NT = (((1,), (1,)), ((), ()))
F32 = jnp.float32
BF16 = jnp.bfloat16


def remote(src, dst, send_sem, recv_sem, tok, pb):
    return pltpu.make_async_remote_copy(
        src_ref=src,
        dst_ref=dst,
        send_sem=send_sem,
        recv_sem=recv_sem,
        device_id=(tok, pb),
        device_id_type=MESH,
    )


def drain(ref, sem):
    pltpu.make_async_copy(ref, ref, sem).wait()


def split_slots(numbers):
    quotient = jnp.floor((numbers + 0.5) * (1.0 / SLOTS))
    return quotient, numbers - SLOTS * quotient


def hop_of(t):
    return jnp.where(t == 0, 2, jnp.where(t == 1, 1, jnp.where(t == 2, 3, 0)))


def kernel(
    act_hbm,
    grad_hbm,
    win_hbm,
    wout_hbm,
    starts_hbm,
    owner_hbm,
    q_hbm,
    out_ref,
    tokens,
    weights,
    docs_ref,
    proj_send,
    proj_own,
    proj_recv,
    proj_relay,
    onehot_ref,
    place,
    lhs,
    rhs,
    wnd,
    wnd_recv,
    units,
    va,
    vb,
    q_all,
    qa_t,
    qb_t,
    fa,
    fb,
    fa_recv,
    fb_recv,
    load_sem,
    w_sem,
    docs_sem,
    q_sem,
    qs_send,
    qs_recv,
    p_send,
    relay_recv,
    p_recv,
    d_send,
    d_recv,
    u_send,
    u_recv,
    f_send,
    f_recv,
    round_sem,
):
    tok = lax.axis_index("tok")
    pb = lax.axis_index("pb")
    z, y, c = tok // 8, (tok // 2) % 4, tok % 2
    me = tok * 4 + pb

    depth_in = act_hbm.shape[1]
    depth_out = grad_hbm.shape[1]
    of_act, of_grad = pl.ds(0, depth_in), pl.ds(depth_in, depth_out)

    def loads_of(hop, half, t, at, sem):
        rows = pl.ds(pl.multiple_of(lax.rem(pb + hop, 4) * SHARE + half * HALF, HALF), HALF)
        return [
            pltpu.make_async_copy(grad_hbm.at[rows], tokens.at[t, at, of_grad], load_sem.at[sem]),
            pltpu.make_async_copy(act_hbm.at[rows], tokens.at[t, at, of_act], load_sem.at[sem]),
        ]

    def far_half(s):
        return pl.ds(pl.multiple_of(s * HALF, HALF), HALF)

    first_half, second_half = pl.ds(0, HALF), pl.ds(HALF, HALF)

    def full_loads(t):
        return loads_of(jnp.where(t == 3, 0, 1), jnp.where(t == 1, 1, 0), t, first_half, t + 1) + loads_of(
            jnp.where(t == 3, 0, 3), jnp.where(t == 1, 0, 1), t, second_half, t + 1
        )

    small = [
        pltpu.make_async_copy(wout_hbm, weights.at[pl.ds(64, 64), of_grad], w_sem),
        pltpu.make_async_copy(win_hbm, weights.at[pl.ds(0, 64), of_act], w_sem),
        pltpu.make_async_copy(starts_hbm, docs_ref.at[0], docs_sem),
        pltpu.make_async_copy(owner_hbm, docs_ref.at[1], docs_sem),
    ]
    q_loads = [
        pltpu.make_async_copy(q_hbm.at[pl.ds(0, 1024)], q_all.at[0, y], q_sem),
        pltpu.make_async_copy(q_hbm.at[pl.ds(1024, 1024)], q_all.at[1, z], q_sem),
    ]
    small[0].start()
    small[1].start()
    for copy in loads_of(2, 0, 0, first_half, 0) + q_loads + loads_of(2, 1, 0, second_half, 1):
        copy.start()

    @pl.loop(1, 4)
    def _(t):
        for copy in full_loads(t):
            copy.start()

    small[2].start()
    small[3].start()

    planes = [lax.rem(pb + n, 4) for n in range(4)]
    on_y = [z * 8 + lax.rem(y + n, 4) * 2 + c for n in range(1, 4)]
    on_z = [lax.rem(z + n, 4) * 8 + y * 2 + c for n in range(1, 4)]
    on_core = [z * 8 + y * 2 + 1 - c]

    def signal(sem, toks):
        for to in toks:
            pl.semaphore_signal(sem, inc=1, device_id=(to, pb), device_id_type=MESH)

    barrier = pltpu.get_barrier_semaphore()
    for plane in planes[1:]:
        pl.semaphore_signal(barrier, inc=1, device_id=(tok, plane), device_id_type=MESH)
    signal(barrier, on_y + on_z + on_core)

    q_first, q_second, q_passed = [], [], []
    for h, place_me in enumerate((y, z)):
        right, left = lax.rem(place_me + 1, 4), lax.rem(place_me + 3, 4)
        for k, (to, row, src, group) in enumerate(
            (
                (right, 0, place_me, q_first),
                (left, 512, place_me, q_first),
                (right, 512, place_me, q_second),
                (left, 0, place_me, q_second),
                (right, 0, left, q_passed),
                (left, 512, right, q_passed),
            )
        ):
            part = q_all.at[h, src, pl.ds(row, 512)]
            to_tok = z * 8 + to * 2 + c if h == 0 else to * 8 + y * 2 + c
            group.append(remote(part, part, qs_send, qs_recv.at[0 if k < 2 else 1], to_tok, pb))

    weights[:64, depth_in:] = jnp.zeros((64, depth_out), BF16)
    weights[64:, :depth_in] = jnp.zeros((64, depth_in), BF16)
    drain(weights.at[pl.ds(0, 64)], w_sem)

    def project(t, at):
        return lax.dot_general(tokens[t, at, :], weights[...], NT, preferred_element_type=F32)

    def relay_copy(s):
        return remote(
            proj_send.at[0, far_half(s)],
            proj_relay.at[far_half(s)],
            p_send,
            relay_recv,
            tok,
            lax.rem(pb + 1 + 2 * s, 4),
        )

    def proj_copies(t):
        return [
            remote(
                proj_send.at[t, at],
                proj_recv.at[n, pl.ds(pl.multiple_of(half * HALF, HALF), HALF)],
                p_send,
                p_recv,
                tok,
                lax.rem(pb + 1 + 2 * n, 4),
            )
            for n, at, half in ((0, first_half, 2 - t), (1, second_half, t - 1))
        ]

    @pl.loop(0, 2)
    def _(s):
        drain(tokens.at[0, far_half(s)], load_sem.at[s])
        proj_send[0, far_half(s), :] = project(0, far_half(s)).astype(BF16)

        @pl.when(s == 0)
        def _():
            pl.semaphore_wait(barrier, 10)
            signal(round_sem.at[0], on_y)

        relay_copy(s).start()

        @pl.when(s == 0)
        def _():
            drain(q_all.at[0, pl.ds(0, 2)], q_sem)
            for copy in q_first + q_second:
                copy.start()

    @pl.loop(1, 4)
    def _(t):
        drain(tokens.at[t], load_sem.at[t + 1])
        both = project(t, pl.ds(0, SHARE))

        @pl.when(t == 1)
        def _():
            proj_send[1] = both.astype(BF16)

        @pl.when(t == 2)
        def _():
            drain(proj_relay, relay_recv)
            proj_send[2] = (both + proj_relay[...].astype(F32)).astype(BF16)

        @pl.when(t < 3)
        def _():
            for copy in proj_copies(t):
                copy.start()

        @pl.when(t == 1)
        def _():
            pl.semaphore_wait(round_sem.at[0], 3)
            signal(round_sem.at[1], on_z)

        @pl.when(t == 2)
        def _():
            pl.semaphore_wait(round_sem.at[1], 3)
            signal(round_sem.at[2], on_core)

        @pl.when(t == 3)
        def _():
            proj_own[...] = both

    pl.semaphore_wait(round_sem.at[2], 1)
    drain(q_all.at[0, pl.ds(0, 2)], qs_recv.at[0])
    for copy in q_passed:
        copy.start()

    drain(docs_ref, docs_sem)
    starts = docs_ref[0]
    begun = starts <= me * SHARE + lax.broadcasted_iota(jnp.int32, (SHARE, 512), 0)
    doc = lax.broadcasted_iota(jnp.int32, (8, 512), 1).astype(F32)
    doc_slot = split_slots(doc)[1]
    slot_before = jnp.where(doc > 0, split_slots(doc - 1)[1], -1.0)
    row_block, row_slot = split_slots(lax.broadcasted_iota(jnp.int32, (GROUP, 128), 0).astype(F32))
    slot_row = row_slot[:, 0:1]
    enters = (doc_slot[0:1, :] == slot_row).astype(F32) - (slot_before[0:1, :] == slot_row).astype(F32)
    onehot_ref[...] = lax.dot_general(
        enters.astype(BF16), begun.astype(F32).astype(BF16), NT, preferred_element_type=F32
    )

    drain(proj_recv, p_recv)
    proj = proj_own[...]
    for t in range(2):
        proj = proj + proj_recv[t].astype(F32)
    proj = proj.astype(BF16)

    onehot = onehot_ref[...]
    lane = lax.broadcasted_iota(jnp.int32, (GROUP, 128), 1)
    low = lax.broadcasted_iota(jnp.int32, (SHARE, 128), 1) < 64
    wide = proj.astype(F32)
    rhs[...] = jnp.concatenate(
        [jnp.where(low, wide, 0.0), jnp.where(low, 0.0, pltpu.roll(wide, 64, 1))], axis=0
    ).astype(BF16)
    mine = pl.ds(lax.rem(me, 32) * PAIRS, PAIRS)
    far_planes = [planes[2], planes[1], planes[3], planes[0]]

    def send_block(to, plane):
        remote(
            wnd.at[pl.ds(to * PAIRS, PAIRS)],
            wnd_recv.at[z, mine],
            d_send,
            d_recv.at[z],
            to,
            plane,
        ).start()

    @pl.loop(0, 4)
    def _(k):
        g = lax.rem(z + hop_of(k), 4)
        first_r = (64 + g * 16).astype(F32) + 2 * row_block
        for half in range(2):
            pick = (lane.astype(F32) == first_r + half).astype(F32).astype(BF16)
            of_row = lax.dot_general(pick, proj, NT, preferred_element_type=F32)
            lhs[:, pl.ds(half * SHARE, SHARE)] = (onehot * of_row).astype(BF16)
        sums = jnp.dot(lhs[...], rhs[...], preferred_element_type=F32)
        wnd[pl.ds(g * 8 * PAIRS, 8 * PAIRS)] = sums.astype(BF16).reshape(8 * PAIRS, 2, 128)

        @pl.loop(0, 3)
        def _(n):
            row = g * 8 + lax.rem(y + hop_of(n), 4) * 2
            for plane in far_planes:
                send_block(row + c, plane)
                send_block(row + 1 - c, plane)

        for plane in far_planes[:3]:
            send_block(g * 8 + y * 2 + c, plane)
            send_block(g * 8 + y * 2 + 1 - c, plane)
        send_block(g * 8 + y * 2 + 1 - c, pb)

        @pl.when(k < 3)
        def _():
            send_block(g * 8 + y * 2 + c, pb)

    wnd_recv[z, mine] = wnd[pl.ds(tok * PAIRS, PAIRS)]
    lane8 = lax.broadcasted_iota(jnp.int32, (8, 512), 1)
    row8 = lax.broadcasted_iota(jnp.int32, (8, 512), 0)
    first = jnp.broadcast_to(starts, (8, 512)) // SHARE
    last = jnp.where(lane8 == 511, DEVICES - 1, pltpu.roll(first, 511, 1))
    facts = jnp.where(row8 == 0, first.astype(F32), jnp.where(row8 == 1, last.astype(F32), doc_slot))
    rank = docs_ref[1] * 16 + lax.broadcasted_iota(jnp.int32, (1, 512), 1) // 32
    perm = (rank == lax.broadcasted_iota(jnp.int32, (512, 512), 0)).astype(F32).astype(BF16)
    ranked = lax.dot_general(perm, facts.astype(BF16), NT, preferred_element_type=F32)
    block, slot = split_slots(lax.broadcasted_iota(jnp.int32, (8, 32 * SLOTS), 1).astype(F32))
    block = block[0:1, :]
    own_slot = ranked[:, 2:3] == slot[0:1, :]

    @pl.loop(0, 4)
    def _(g):
        from_block = ranked[:, 0:1] - (g * 32).astype(F32)
        to_block = ranked[:, 1:2] - (g * 32).astype(F32)
        inside = (from_block <= block) & (block <= to_block) & own_slot
        place[g] = inside.astype(F32).astype(BF16)

    summed = jnp.zeros((512, 128), F32)
    for n in (2, 3, 1, 0):
        g = (z + n) % 4
        got = wnd_recv.at[g, pl.ds(0, (32 if n else 31) * PAIRS)]
        drain(got, d_recv.at[g])
        summed = summed + jnp.dot(
            place[g], wnd_recv[g].reshape(32 * SLOTS, 128), preferred_element_type=F32
        )
    units[...] = summed.astype(BF16).reshape(4, 4, 32, 128)

    at_y = pl.ds(pl.multiple_of(y * 128, 128), 128)
    at_z = pl.ds(pl.multiple_of(z * 128, 128), 128)
    u_copies = []
    for n in range(1, 4):
        ty, tz = (y + n) % 4, (z + n) % 4
        u_copies.append(
            remote(
                units.at[tz], vb.at[:, :, at_z], u_send, u_recv.at[1], tz * 8 + y * 2 + c, pb
            )
        )
        u_copies.append(
            remote(
                units.at[:, ty], va.at[:, :, at_y], u_send, u_recv.at[0], z * 8 + ty * 2 + c, pb
            )
        )
    for copy in u_copies:
        copy.start()
    va[:, :, at_y] = units[:, y]
    vb[:, :, at_z] = units[z]
    fa_me, fb_me = z * 2 + c, y * 2 + c

    drain(q_all.at[0], qs_recv.at[1])
    for n in range(4):
        qa_t[pl.ds(n * 128, 128), :] = q_all[0, n].T
        qb_t[pl.ds(n * 128, 128), :] = q_all[1, n].T

    drain(vb.at[:, :, pl.ds(0, 384)], u_recv.at[1])
    fb[...] = jnp.dot(vb[...].reshape(128, 512), qb_t[...], preferred_element_type=F32).astype(BF16)

    @pl.loop(1, 8)
    def _(n):
        to = (fb_me + n) % 8
        remote(
            fb.at[pl.ds(pl.multiple_of(to * 16, 16), 16)],
            fb_recv.at[fb_me],
            f_send,
            f_recv.at[1],
            z * 8 + to,
            pb,
        ).start()

    drain(va.at[:, :, pl.ds(0, 384)], u_recv.at[0])
    docs = va[...].reshape(128, 512)
    fa[:, :1024] = jnp.dot(docs, qa_t[...], preferred_element_type=F32).astype(BF16)
    wide = docs.astype(F32)
    square = jnp.broadcast_to(jnp.sum(wide * wide, axis=1, keepdims=True), (128, 128))
    high = square.astype(BF16).astype(F32)
    fa[:, 1024:] = jnp.where(
        lax.broadcasted_iota(jnp.int32, (128, 128), 1) < 64, high, square - high
    ).astype(BF16)

    @pl.loop(1, 8)
    def _(n):
        to = (fa_me + n) % 8
        remote(
            fa.at[pl.ds(pl.multiple_of(to * 16, 16), 16)],
            fa_recv.at[fa_me],
            f_send,
            f_recv.at[0],
            (to // 2) * 8 + y * 2 + to % 2,
            pb,
        ).start()

    fa_recv[fa_me] = fa[pl.ds(pl.multiple_of(fa_me * 16, 16), 16), :]
    fb_recv[fb_me] = fb[pl.ds(pl.multiple_of(fb_me * 16, 16), 16), :]
    drain(fb_recv.at[pl.ds(0, 7)], f_recv.at[1])
    total_b = fb_recv[0].astype(F32)
    for n in range(1, 8):
        total_b = total_b + fb_recv[n].astype(F32)
    drain(fa_recv.at[pl.ds(0, 7)], f_recv.at[0])
    total_a = fa_recv[0].astype(F32)
    for n in range(1, 8):
        total_a = total_a + fa_recv[n].astype(F32)
    tail = total_a[:, 1024:]
    norm = lax.rsqrt(tail + pltpu.roll(tail, 64, 1) + EPS)[:, 0:1]
    out_ref[:, :1024] = total_a[:, :1024] * norm
    out_ref[:, 1024:] = total_b * norm

    drain(proj_send, p_send)
    drain(q_all.at[:, pl.ds(0, 3)], qs_send)
    for n in range(2):
        drain(va.at[:, :, pl.ds(0, 384)], u_send)
    for g in range(4):
        drain(wnd.at[pl.ds(0, (32 if g else 31) * PAIRS)], d_send)
    drain(fa.at[pl.ds(0, 112)], f_send)
    drain(fb.at[pl.ds(0, 112)], f_send)


def per_device(activations, out_grads, proj_in, proj_out, doc_starts, doc_owner, queries):
    depth_in, depth_out = activations.shape[1], out_grads.shape[1]
    dma = pltpu.SemaphoreType.DMA
    vmem = pltpu.VMEM

    def on_hbm(array):
        return pltpu.with_memory_space_constraint(array, pltpu.HBM)

    return pl.pallas_call(
        kernel,
        out_shape=jax.ShapeDtypeStruct((16, 2048), F32),
        in_specs=[pl.BlockSpec(memory_space=pltpu.HBM)] * 7,
        out_specs=pl.BlockSpec(memory_space=pltpu.VMEM),
        scratch_shapes=[
            vmem((4, SHARE, depth_in + depth_out), BF16),
            vmem((128, depth_in + depth_out), BF16),
            vmem((2, 1, 512), jnp.int32),
            vmem((3, SHARE, 128), BF16),
            vmem((SHARE, 128), F32),
            vmem((2, SHARE, 128), BF16),
            vmem((SHARE, 128), BF16),
            vmem((GROUP, SHARE), F32),
            vmem((4, 512, 32 * SLOTS), BF16),
            vmem((GROUP, 2 * SHARE), BF16),
            vmem((2 * SHARE, 128), BF16),
            vmem((32 * PAIRS, 2, 128), BF16),
            vmem((4, 32 * PAIRS, 2, 128), BF16),
            vmem((4, 4, 32, 128), BF16),
            vmem((4, 32, 512), BF16),
            vmem((4, 32, 512), BF16),
            vmem((2, 4, 1024, 128), BF16),
            vmem((512, 1024), BF16),
            vmem((512, 1024), BF16),
            vmem((128, 1152), BF16),
            vmem((128, 1024), BF16),
            vmem((8, 16, 1152), BF16),
            vmem((8, 16, 1024), BF16),
            dma((5,)),
            dma,
            dma,
            dma,
            dma,
            dma((2,)),
            dma,
            dma,
            dma,
            dma,
            dma((4,)),
            dma,
            dma((2,)),
            dma,
            dma((2,)),
            pltpu.SemaphoreType.REGULAR((3,)),
        ],
        compiler_params=pltpu.CompilerParams(
            collective_id=0, has_side_effects=True, vmem_limit_bytes=48 * 1024 * 1024
        ),
    )(
        on_hbm(activations),
        on_hbm(out_grads),
        on_hbm(proj_in.T),
        on_hbm(proj_out.T),
        on_hbm(doc_starts.reshape(1, 512)),
        on_hbm(doc_owner.reshape(1, 512)),
        on_hbm(queries),
    )


def solution(mesh):
    in_specs = (
        P("tok", "pb"),
        P("tok", "pb"),
        P("pb", None),
        P("pb", None),
        P(),
        P(),
        P("pb", "tok"),
    )
    return jax.shard_map(
        per_device, mesh=mesh, in_specs=in_specs, out_specs=P("tok", "pb"), check_vma=False
    )
```

```python
import functools

import jax
import jax.numpy as jnp
from jax import lax
from jax.experimental import pallas as pl
from jax.experimental.pallas import tpu as pltpu
from jax.sharding import PartitionSpec as P

EPS = 1e-06
SHARE = 512
SLOTS = 10
PAIRS = SLOTS // 2
GROUP = 8 * SLOTS
MESH = pl.DeviceIdType.MESH
DEVICES = 128
HALF = 256
NT = (((1,), (1,)), ((), ()))
F32 = jnp.float32
BF16 = jnp.bfloat16


def remote(src, dst, send_sem, recv_sem, tok, pb):
    return pltpu.make_async_remote_copy(
        src_ref=src,
        dst_ref=dst,
        send_sem=send_sem,
        recv_sem=recv_sem,
        device_id=(tok, pb),
        device_id_type=MESH,
    )


def drain(ref, sem):
    pltpu.make_async_copy(ref, ref, sem).wait()


def split_slots(numbers):
    quotient = jnp.floor((numbers + 0.5) * (1.0 / SLOTS))
    return quotient, numbers - SLOTS * quotient


def hop_of(t):
    return jnp.where(t == 0, 2, jnp.where(t == 1, 1, jnp.where(t == 2, 3, 0)))


def kernel(
    act_hbm,
    grad_hbm,
    win_hbm,
    wout_hbm,
    starts_hbm,
    owner_hbm,
    q_hbm,
    out_ref,
    tokens,
    weights,
    docs_ref,
    proj_send,
    proj_own,
    proj_recv,
    proj_relay,
    onehot_ref,
    place,
    lhs,
    rhs,
    wnd,
    wnd_recv,
    units,
    va,
    vb,
    q_all,
    qa_t,
    qb_t,
    fa,
    fb,
    fa_recv,
    fb_recv,
    load_sem,
    w_sem,
    docs_sem,
    q_sem,
    qs_send,
    qs_recv,
    p_send,
    relay_recv,
    p_recv,
    d_send,
    d_recv,
    u_send,
    u_recv,
    f_send,
    f_recv,
    round_sem,
):
    tok = lax.axis_index("tok")
    pb = lax.axis_index("pb")
    z, y, c = tok // 8, (tok // 2) % 4, tok % 2
    me = tok * 4 + pb

    depth_in = act_hbm.shape[1]
    depth_out = grad_hbm.shape[1]
    of_act, of_grad = pl.ds(0, depth_in), pl.ds(depth_in, depth_out)

    def loads_of(hop, half, t, at, sem):
        rows = pl.ds(pl.multiple_of(lax.rem(pb + hop, 4) * SHARE + half * HALF, HALF), HALF)
        return [
            pltpu.make_async_copy(grad_hbm.at[rows], tokens.at[t, at, of_grad], load_sem.at[sem]),
            pltpu.make_async_copy(act_hbm.at[rows], tokens.at[t, at, of_act], load_sem.at[sem]),
        ]

    def far_half(s):
        return pl.ds(pl.multiple_of(s * HALF, HALF), HALF)

    first_half, second_half = pl.ds(0, HALF), pl.ds(HALF, HALF)

    def full_loads(t):
        return loads_of(jnp.where(t == 3, 0, 1), jnp.where(t == 1, 1, 0), t, first_half, t + 1) + loads_of(
            jnp.where(t == 3, 0, 3), jnp.where(t == 1, 0, 1), t, second_half, t + 1
        )

    small = [
        pltpu.make_async_copy(wout_hbm, weights.at[pl.ds(64, 64), of_grad], w_sem),
        pltpu.make_async_copy(win_hbm, weights.at[pl.ds(0, 64), of_act], w_sem),
        pltpu.make_async_copy(starts_hbm, docs_ref.at[0], docs_sem),
        pltpu.make_async_copy(owner_hbm, docs_ref.at[1], docs_sem),
    ]
    q_loads = [
        pltpu.make_async_copy(q_hbm.at[pl.ds(0, 1024)], q_all.at[0, y], q_sem),
        pltpu.make_async_copy(q_hbm.at[pl.ds(1024, 1024)], q_all.at[1, z], q_sem),
    ]
    small[0].start()
    small[1].start()
    for copy in loads_of(2, 0, 0, first_half, 0) + q_loads + loads_of(2, 1, 0, second_half, 1):
        copy.start()

    @pl.loop(1, 4)
    def _(t):
        for copy in full_loads(t):
            copy.start()

    small[2].start()
    small[3].start()

    planes = [lax.rem(pb + n, 4) for n in range(4)]
    on_y = [z * 8 + lax.rem(y + n, 4) * 2 + c for n in range(1, 4)]
    on_z = [lax.rem(z + n, 4) * 8 + y * 2 + c for n in range(1, 4)]
    on_core = [z * 8 + y * 2 + 1 - c]

    def signal(sem, toks):
        for to in toks:
            pl.semaphore_signal(sem, inc=1, device_id=(to, pb), device_id_type=MESH)

    barrier = pltpu.get_barrier_semaphore()
    for plane in planes[1:]:
        pl.semaphore_signal(barrier, inc=1, device_id=(tok, plane), device_id_type=MESH)
    signal(barrier, on_y + on_z + on_core)

    q_first, q_second, q_passed = [], [], []
    for h, place_me in enumerate((y, z)):
        right, left = lax.rem(place_me + 1, 4), lax.rem(place_me + 3, 4)
        for k, (to, row, src, group) in enumerate(
            (
                (right, 0, place_me, q_first),
                (left, 512, place_me, q_first),
                (right, 512, place_me, q_second),
                (left, 0, place_me, q_second),
                (right, 0, left, q_passed),
                (left, 512, right, q_passed),
            )
        ):
            part = q_all.at[h, src, pl.ds(row, 512)]
            to_tok = z * 8 + to * 2 + c if h == 0 else to * 8 + y * 2 + c
            group.append(remote(part, part, qs_send, qs_recv.at[0 if k < 2 else 1], to_tok, pb))

    weights[:64, depth_in:] = jnp.zeros((64, depth_out), BF16)
    weights[64:, :depth_in] = jnp.zeros((64, depth_in), BF16)
    drain(weights.at[pl.ds(0, 64)], w_sem)

    def project(t, at):
        return lax.dot_general(tokens[t, at, :], weights[...], NT, preferred_element_type=F32)

    def relay_copy(s):
        return remote(
            proj_send.at[0, far_half(s)],
            proj_relay.at[far_half(s)],
            p_send,
            relay_recv,
            tok,
            lax.rem(pb + 2, 4),
        )

    def proj_copies(t):
        return [
            remote(
                proj_send.at[t, at],
                proj_recv.at[n, pl.ds(pl.multiple_of(half * HALF, HALF), HALF)],
                p_send,
                p_recv,
                tok,
                lax.rem(pb + 1 + 2 * n, 4),
            )
            for n, at, half in ((0, first_half, 2 - t), (1, second_half, t - 1))
        ]

    @pl.loop(0, 2)
    def _(s):
        drain(tokens.at[0, far_half(s)], load_sem.at[s])
        proj_send[0, far_half(s), :] = project(0, far_half(s)).astype(BF16)

        @pl.when(s == 0)
        def _():
            pl.semaphore_wait(barrier, 10)
            signal(round_sem.at[0], on_y)

        relay_copy(s).start()

        @pl.when(s == 0)
        def _():
            drain(q_all.at[0, pl.ds(0, 2)], q_sem)
            for copy in q_first + q_second:
                copy.start()

    @pl.loop(1, 4)
    def _(t):
        drain(tokens.at[t], load_sem.at[t + 1])
        both = project(t, pl.ds(0, SHARE))

        @pl.when(t < 3)
        def _():
            proj_send[t] = both.astype(BF16)
            for copy in proj_copies(t):
                copy.start()

        @pl.when(t == 1)
        def _():
            pl.semaphore_wait(round_sem.at[0], 3)
            signal(round_sem.at[1], on_z)

        @pl.when(t == 2)
        def _():
            pl.semaphore_wait(round_sem.at[1], 3)
            signal(round_sem.at[2], on_core)

        @pl.when(t == 3)
        def _():
            proj_own[...] = both

    pl.semaphore_wait(round_sem.at[2], 1)
    drain(q_all.at[0, pl.ds(0, 2)], qs_recv.at[0])
    for copy in q_passed:
        copy.start()

    drain(docs_ref, docs_sem)
    starts = docs_ref[0]
    begun = starts <= me * SHARE + lax.broadcasted_iota(jnp.int32, (SHARE, 512), 0)
    doc = lax.broadcasted_iota(jnp.int32, (8, 512), 1).astype(F32)
    doc_slot = split_slots(doc)[1]
    slot_before = jnp.where(doc > 0, split_slots(doc - 1)[1], -1.0)
    row_block, row_slot = split_slots(lax.broadcasted_iota(jnp.int32, (GROUP, 128), 0).astype(F32))
    slot_row = row_slot[:, 0:1]
    enters = (doc_slot[0:1, :] == slot_row).astype(F32) - (slot_before[0:1, :] == slot_row).astype(F32)
    onehot_ref[...] = lax.dot_general(
        enters.astype(BF16), begun.astype(F32).astype(BF16), NT, preferred_element_type=F32
    )

    drain(proj_relay, relay_recv)
    proj = proj_own[...] + proj_relay[...].astype(F32)
    drain(proj_recv, p_recv)
    for t in range(2):
        proj = proj + proj_recv[t].astype(F32)
    proj = proj.astype(BF16)

    onehot = onehot_ref[...]
    lane = lax.broadcasted_iota(jnp.int32, (GROUP, 128), 1)
    low = lax.broadcasted_iota(jnp.int32, (SHARE, 128), 1) < 64
    wide = proj.astype(F32)
    rhs[...] = jnp.concatenate(
        [jnp.where(low, wide, 0.0), jnp.where(low, 0.0, pltpu.roll(wide, 64, 1))], axis=0
    ).astype(BF16)
    mine = pl.ds(lax.rem(me, 32) * PAIRS, PAIRS)
    far_planes = [planes[2], planes[1], planes[3], planes[0]]

    def send_block(to, plane):
        remote(
            wnd.at[pl.ds(to * PAIRS, PAIRS)],
            wnd_recv.at[z, mine],
            d_send,
            d_recv.at[z],
            to,
            plane,
        ).start()

    @pl.loop(0, 4)
    def _(k):
        g = lax.rem(z + hop_of(k), 4)
        first_r = (64 + g * 16).astype(F32) + 2 * row_block
        for half in range(2):
            pick = (lane.astype(F32) == first_r + half).astype(F32).astype(BF16)
            of_row = lax.dot_general(pick, proj, NT, preferred_element_type=F32)
            lhs[:, pl.ds(half * SHARE, SHARE)] = (onehot * of_row).astype(BF16)
        sums = jnp.dot(lhs[...], rhs[...], preferred_element_type=F32)
        wnd[pl.ds(g * 8 * PAIRS, 8 * PAIRS)] = sums.astype(BF16).reshape(8 * PAIRS, 2, 128)

        @pl.loop(0, 3)
        def _(n):
            row = g * 8 + lax.rem(y + hop_of(n), 4) * 2
            for plane in far_planes:
                send_block(row + c, plane)
                send_block(row + 1 - c, plane)

        for plane in far_planes[:3]:
            send_block(g * 8 + y * 2 + c, plane)
            send_block(g * 8 + y * 2 + 1 - c, plane)
        send_block(g * 8 + y * 2 + 1 - c, pb)

        @pl.when(k < 3)
        def _():
            send_block(g * 8 + y * 2 + c, pb)

    wnd_recv[z, mine] = wnd[pl.ds(tok * PAIRS, PAIRS)]
    lane8 = lax.broadcasted_iota(jnp.int32, (8, 512), 1)
    row8 = lax.broadcasted_iota(jnp.int32, (8, 512), 0)
    first = jnp.broadcast_to(starts, (8, 512)) // SHARE
    last = jnp.where(lane8 == 511, DEVICES - 1, pltpu.roll(first, 511, 1))
    facts = jnp.where(row8 == 0, first.astype(F32), jnp.where(row8 == 1, last.astype(F32), doc_slot))
    rank = docs_ref[1] * 16 + lax.broadcasted_iota(jnp.int32, (1, 512), 1) // 32
    perm = (rank == lax.broadcasted_iota(jnp.int32, (512, 512), 0)).astype(F32).astype(BF16)
    ranked = lax.dot_general(perm, facts.astype(BF16), NT, preferred_element_type=F32)
    block, slot = split_slots(lax.broadcasted_iota(jnp.int32, (8, 32 * SLOTS), 1).astype(F32))
    block = block[0:1, :]
    own_slot = ranked[:, 2:3] == slot[0:1, :]

    @pl.loop(0, 4)
    def _(g):
        from_block = ranked[:, 0:1] - (g * 32).astype(F32)
        to_block = ranked[:, 1:2] - (g * 32).astype(F32)
        inside = (from_block <= block) & (block <= to_block) & own_slot
        place[g] = inside.astype(F32).astype(BF16)

    summed = jnp.zeros((512, 128), F32)
    for n in (2, 3, 1, 0):
        g = (z + n) % 4
        got = wnd_recv.at[g, pl.ds(0, (32 if n else 31) * PAIRS)]
        drain(got, d_recv.at[g])
        summed = summed + jnp.dot(
            place[g], wnd_recv[g].reshape(32 * SLOTS, 128), preferred_element_type=F32
        )
    units[...] = summed.astype(BF16).reshape(4, 4, 32, 128)

    at_y = pl.ds(pl.multiple_of(y * 128, 128), 128)
    at_z = pl.ds(pl.multiple_of(z * 128, 128), 128)
    def other(n, mine):
        return n + jnp.where(n >= mine, 1, 0)

    u_copies = []
    for n in range(3):
        ty, tz = other(n, y), other(n, z)
        u_copies.append(
            remote(
                units.at[:, ty], va.at[:, :, at_y], u_send, u_recv.at[0], z * 8 + ty * 2 + c, pb
            )
        )
        u_copies.append(
            remote(
                units.at[tz], vb.at[:, :, at_z], u_send, u_recv.at[1], tz * 8 + y * 2 + c, pb
            )
        )
    for copy in u_copies:
        copy.start()
    va[:, :, at_y] = units[:, y]
    vb[:, :, at_z] = units[z]
    fa_me, fb_me = z * 2 + c, y * 2 + c

    drain(q_all.at[0], qs_recv.at[1])
    for n in range(4):
        qa_t[pl.ds(n * 128, 128), :] = q_all[0, n].T
        qb_t[pl.ds(n * 128, 128), :] = q_all[1, n].T

    drain(va.at[:, :, pl.ds(0, 384)], u_recv.at[0])
    docs = va[...].reshape(128, 512)
    fa[:, :1024] = jnp.dot(docs, qa_t[...], preferred_element_type=F32).astype(BF16)
    wide = docs.astype(F32)
    square = jnp.broadcast_to(jnp.sum(wide * wide, axis=1, keepdims=True), (128, 128))
    high = square.astype(BF16).astype(F32)
    fa[:, 1024:] = jnp.where(
        lax.broadcasted_iota(jnp.int32, (128, 128), 1) < 64, high, square - high
    ).astype(BF16)

    @pl.loop(0, 7)
    def _(n):
        to = other(n, fa_me)
        remote(
            fa.at[pl.ds(pl.multiple_of(to * 16, 16), 16)],
            fa_recv.at[fa_me],
            f_send,
            f_recv.at[0],
            lax.div(to, 2) * 8 + y * 2 + lax.rem(to, 2),
            pb,
        ).start()

    drain(vb.at[:, :, pl.ds(0, 384)], u_recv.at[1])
    fb[...] = jnp.dot(vb[...].reshape(128, 512), qb_t[...], preferred_element_type=F32).astype(BF16)

    @pl.loop(0, 7)
    def _(n):
        to = other(n, fb_me)
        remote(
            fb.at[pl.ds(pl.multiple_of(to * 16, 16), 16)],
            fb_recv.at[fb_me],
            f_send,
            f_recv.at[1],
            z * 8 + to,
            pb,
        ).start()

    fa_recv[fa_me] = fa[pl.ds(pl.multiple_of(fa_me * 16, 16), 16), :]
    fb_recv[fb_me] = fb[pl.ds(pl.multiple_of(fb_me * 16, 16), 16), :]
    drain(fa_recv.at[pl.ds(0, 7)], f_recv.at[0])
    total_a = fa_recv[0].astype(F32)
    for n in range(1, 8):
        total_a = total_a + fa_recv[n].astype(F32)
    tail = total_a[:, 1024:]
    norm = lax.rsqrt(tail + pltpu.roll(tail, 64, 1) + EPS)[:, 0:1]
    out_ref[:, :1024] = total_a[:, :1024] * norm
    drain(fb_recv.at[pl.ds(0, 7)], f_recv.at[1])
    total_b = fb_recv[0].astype(F32)
    for n in range(1, 8):
        total_b = total_b + fb_recv[n].astype(F32)
    out_ref[:, 1024:] = total_b * norm

    drain(proj_send, p_send)
    drain(q_all.at[:, pl.ds(0, 3)], qs_send)
    for n in range(2):
        drain(va.at[:, :, pl.ds(0, 384)], u_send)
    for g in range(4):
        drain(wnd.at[pl.ds(0, (32 if g else 31) * PAIRS)], d_send)
    drain(fa.at[pl.ds(0, 112)], f_send)
    drain(fb.at[pl.ds(0, 112)], f_send)


def per_device(activations, out_grads, proj_in, proj_out, doc_starts, doc_owner, queries):
    depth_in, depth_out = activations.shape[1], out_grads.shape[1]
    dma = pltpu.SemaphoreType.DMA
    vmem = pltpu.VMEM

    def on_hbm(array):
        return pltpu.with_memory_space_constraint(array, pltpu.HBM)

    return pl.pallas_call(
        kernel,
        out_shape=jax.ShapeDtypeStruct((16, 2048), F32),
        in_specs=[pl.BlockSpec(memory_space=pltpu.HBM)] * 7,
        out_specs=pl.BlockSpec(memory_space=pltpu.VMEM),
        scratch_shapes=[
            vmem((4, SHARE, depth_in + depth_out), BF16),
            vmem((128, depth_in + depth_out), BF16),
            vmem((2, 1, 512), jnp.int32),
            vmem((3, SHARE, 128), BF16),
            vmem((SHARE, 128), F32),
            vmem((2, SHARE, 128), BF16),
            vmem((SHARE, 128), BF16),
            vmem((GROUP, SHARE), F32),
            vmem((4, 512, 32 * SLOTS), BF16),
            vmem((GROUP, 2 * SHARE), BF16),
            vmem((2 * SHARE, 128), BF16),
            vmem((32 * PAIRS, 2, 128), BF16),
            vmem((4, 32 * PAIRS, 2, 128), BF16),
            vmem((4, 4, 32, 128), BF16),
            vmem((4, 32, 512), BF16),
            vmem((4, 32, 512), BF16),
            vmem((2, 4, 1024, 128), BF16),
            vmem((512, 1024), BF16),
            vmem((512, 1024), BF16),
            vmem((128, 1152), BF16),
            vmem((128, 1024), BF16),
            vmem((8, 16, 1152), BF16),
            vmem((8, 16, 1024), BF16),
            dma((5,)),
            dma,
            dma,
            dma,
            dma,
            dma((2,)),
            dma,
            dma,
            dma,
            dma,
            dma((4,)),
            dma,
            dma((2,)),
            dma,
            dma((2,)),
            pltpu.SemaphoreType.REGULAR((3,)),
        ],
        compiler_params=pltpu.CompilerParams(
            collective_id=0, has_side_effects=True, vmem_limit_bytes=48 * 1024 * 1024
        ),
    )(
        on_hbm(activations),
        on_hbm(out_grads),
        on_hbm(proj_in.T),
        on_hbm(proj_out.T),
        on_hbm(doc_starts.reshape(1, 512)),
        on_hbm(doc_owner.reshape(1, 512)),
        on_hbm(queries),
    )


def solution(mesh):
    in_specs = (
        P("tok", "pb"),
        P("tok", "pb"),
        P("pb", None),
        P("pb", None),
        P(),
        P(),
        P("pb", "tok"),
    )
    return jax.shard_map(
        per_device, mesh=mesh, in_specs=in_specs, out_specs=P("tok", "pb"), check_vma=False
    )
```

```python
import functools

import jax
import jax.numpy as jnp
from jax import lax
from jax.experimental import pallas as pl
from jax.experimental.pallas import tpu as pltpu
from jax.sharding import PartitionSpec as P

EPS = 1e-06
SHARE = 512
SLOTS = 10
PAIRS = SLOTS // 2
GROUP = 8 * SLOTS
MESH = pl.DeviceIdType.MESH
DEVICES = 128
HALF = 256
NT = (((1,), (1,)), ((), ()))
F32 = jnp.float32
BF16 = jnp.bfloat16


def remote(src, dst, send_sem, recv_sem, tok, pb):
    return pltpu.make_async_remote_copy(
        src_ref=src,
        dst_ref=dst,
        send_sem=send_sem,
        recv_sem=recv_sem,
        device_id=(tok, pb),
        device_id_type=MESH,
    )


def drain(ref, sem):
    pltpu.make_async_copy(ref, ref, sem).wait()


def split_slots(numbers):
    quotient = jnp.floor((numbers + 0.5) * (1.0 / SLOTS))
    return quotient, numbers - SLOTS * quotient


def hop_of(t):
    return jnp.where(t == 0, 2, jnp.where(t == 1, 1, jnp.where(t == 2, 3, 0)))


def kernel(
    act_hbm,
    grad_hbm,
    win_hbm,
    wout_hbm,
    starts_hbm,
    owner_hbm,
    q_hbm,
    out_ref,
    tokens,
    weights,
    docs_ref,
    proj_send,
    proj_own,
    proj_recv,
    proj_relay,
    onehot_ref,
    place,
    lhs,
    rhs,
    wnd,
    wnd_recv,
    units,
    va,
    vb,
    q_all,
    qa_t,
    qb_t,
    fa,
    fb,
    fa_recv,
    fb_recv,
    load_sem,
    w_sem,
    docs_sem,
    q_sem,
    qs_send,
    qs_recv,
    p_send,
    relay_recv,
    p_recv,
    d_send,
    d_recv,
    u_send,
    u_recv,
    f_send,
    f_recv,
    round_sem,
):
    tok = lax.axis_index("tok")
    pb = lax.axis_index("pb")
    z, y, c = tok // 8, (tok // 2) % 4, tok % 2
    me = tok * 4 + pb

    depth_in = act_hbm.shape[1]
    depth_out = grad_hbm.shape[1]
    of_act, of_grad = pl.ds(0, depth_in), pl.ds(depth_in, depth_out)

    def loads_of(hop, half, t, at, sem):
        rows = pl.ds(pl.multiple_of(lax.rem(pb + hop, 4) * SHARE + half * HALF, HALF), HALF)
        return [
            pltpu.make_async_copy(grad_hbm.at[rows], tokens.at[t, at, of_grad], load_sem.at[sem]),
            pltpu.make_async_copy(act_hbm.at[rows], tokens.at[t, at, of_act], load_sem.at[sem]),
        ]

    def far_half(s):
        return pl.ds(pl.multiple_of(s * HALF, HALF), HALF)

    first_half, second_half = pl.ds(0, HALF), pl.ds(HALF, HALF)

    def full_loads(t):
        return loads_of(jnp.where(t == 3, 0, 1), jnp.where(t == 1, 1, 0), t, first_half, t + 1) + loads_of(
            jnp.where(t == 3, 0, 3), jnp.where(t == 1, 0, 1), t, second_half, t + 1
        )

    small = [
        pltpu.make_async_copy(wout_hbm, weights.at[pl.ds(64, 64), of_grad], w_sem),
        pltpu.make_async_copy(win_hbm, weights.at[pl.ds(0, 64), of_act], w_sem),
        pltpu.make_async_copy(starts_hbm, docs_ref.at[0], docs_sem),
        pltpu.make_async_copy(owner_hbm, docs_ref.at[1], docs_sem),
    ]
    q_loads = [
        pltpu.make_async_copy(q_hbm.at[pl.ds(0, 1024)], q_all.at[0, y], q_sem),
        pltpu.make_async_copy(q_hbm.at[pl.ds(1024, 1024)], q_all.at[1, z], q_sem),
    ]
    small[0].start()
    small[1].start()
    for copy in loads_of(2, 0, 0, first_half, 0) + q_loads + loads_of(2, 1, 0, second_half, 1):
        copy.start()

    @pl.loop(1, 4)
    def _(t):
        for copy in full_loads(t):
            copy.start()

    small[2].start()
    small[3].start()

    planes = [lax.rem(pb + n, 4) for n in range(4)]
    on_y = [z * 8 + lax.rem(y + n, 4) * 2 + c for n in range(1, 4)]
    on_z = [lax.rem(z + n, 4) * 8 + y * 2 + c for n in range(1, 4)]
    on_core = [z * 8 + y * 2 + 1 - c]

    def signal(sem, toks):
        for to in toks:
            pl.semaphore_signal(sem, inc=1, device_id=(to, pb), device_id_type=MESH)

    barrier = pltpu.get_barrier_semaphore()
    for plane in planes[1:]:
        pl.semaphore_signal(barrier, inc=1, device_id=(tok, plane), device_id_type=MESH)
    signal(barrier, on_y + on_z + on_core)

    q_first, q_second, q_passed = [], [], []
    for h, place_me in enumerate((y, z)):
        right, left = lax.rem(place_me + 1, 4), lax.rem(place_me + 3, 4)
        for k, (to, row, src, group) in enumerate(
            (
                (right, 0, place_me, q_first),
                (left, 512, place_me, q_first),
                (right, 512, place_me, q_second),
                (left, 0, place_me, q_second),
                (right, 0, left, q_passed),
                (left, 512, right, q_passed),
            )
        ):
            part = q_all.at[h, src, pl.ds(row, 512)]
            to_tok = z * 8 + to * 2 + c if h == 0 else to * 8 + y * 2 + c
            group.append(remote(part, part, qs_send, qs_recv.at[0 if k < 2 else 1], to_tok, pb))

    weights[:64, depth_in:] = jnp.zeros((64, depth_out), BF16)
    weights[64:, :depth_in] = jnp.zeros((64, depth_in), BF16)
    drain(weights.at[pl.ds(0, 64)], w_sem)

    def project(t, at):
        return lax.dot_general(tokens[t, at, :], weights[...], NT, preferred_element_type=F32)

    def relay_copy(s):
        return remote(
            proj_send.at[0, far_half(s)],
            proj_relay.at[far_half(s)],
            p_send,
            relay_recv,
            tok,
            lax.rem(pb + 2, 4),
        )

    def proj_copies(t):
        return [
            remote(
                proj_send.at[t, at],
                proj_recv.at[n, pl.ds(pl.multiple_of(half * HALF, HALF), HALF)],
                p_send,
                p_recv,
                tok,
                lax.rem(pb + 1 + 2 * n, 4),
            )
            for n, at, half in ((0, first_half, 2 - t), (1, second_half, t - 1))
        ]

    @pl.loop(0, 2)
    def _(s):
        drain(tokens.at[0, far_half(s)], load_sem.at[s])
        proj_send[0, far_half(s), :] = project(0, far_half(s)).astype(BF16)

        @pl.when(s == 0)
        def _():
            pl.semaphore_wait(barrier, 10)
            signal(round_sem.at[0], on_y)

        relay_copy(s).start()

        @pl.when(s == 0)
        def _():
            drain(q_all.at[0, pl.ds(0, 2)], q_sem)
            for copy in q_first + q_second:
                copy.start()

    @pl.loop(1, 4)
    def _(t):
        drain(tokens.at[t], load_sem.at[t + 1])
        both = project(t, pl.ds(0, SHARE))

        @pl.when(t < 3)
        def _():
            proj_send[t] = both.astype(BF16)
            for copy in proj_copies(t):
                copy.start()

        @pl.when(t == 1)
        def _():
            pl.semaphore_wait(round_sem.at[0], 3)
            signal(round_sem.at[1], on_z)

        @pl.when(t == 2)
        def _():
            pl.semaphore_wait(round_sem.at[1], 3)
            signal(round_sem.at[2], on_core)

        @pl.when(t == 3)
        def _():
            proj_own[...] = both

    pl.semaphore_wait(round_sem.at[2], 1)
    drain(q_all.at[0, pl.ds(0, 2)], qs_recv.at[0])
    for copy in q_passed:
        copy.start()

    drain(docs_ref, docs_sem)
    starts = docs_ref[0]
    begun = starts <= me * SHARE + lax.broadcasted_iota(jnp.int32, (SHARE, 512), 0)
    doc = lax.broadcasted_iota(jnp.int32, (8, 512), 1).astype(F32)
    doc_slot = split_slots(doc)[1]
    slot_before = jnp.where(doc > 0, split_slots(doc - 1)[1], -1.0)
    row_block, row_slot = split_slots(lax.broadcasted_iota(jnp.int32, (GROUP, 128), 0).astype(F32))
    slot_row = row_slot[:, 0:1]
    enters = (doc_slot[0:1, :] == slot_row).astype(F32) - (slot_before[0:1, :] == slot_row).astype(F32)
    onehot_ref[...] = lax.dot_general(
        enters.astype(BF16), begun.astype(F32).astype(BF16), NT, preferred_element_type=F32
    )

    drain(proj_relay, relay_recv)
    proj = proj_own[...] + proj_relay[...].astype(F32)
    drain(proj_recv, p_recv)
    for t in range(2):
        proj = proj + proj_recv[t].astype(F32)
    proj = proj.astype(BF16)

    onehot = onehot_ref[...]
    lane = lax.broadcasted_iota(jnp.int32, (GROUP, 128), 1)
    low = lax.broadcasted_iota(jnp.int32, (SHARE, 128), 1) < 64
    wide = proj.astype(F32)
    rhs[...] = jnp.concatenate(
        [jnp.where(low, wide, 0.0), jnp.where(low, 0.0, pltpu.roll(wide, 64, 1))], axis=0
    ).astype(BF16)
    mine = pl.ds(lax.rem(me, 32) * PAIRS, PAIRS)
    far_planes = [planes[2], planes[1], planes[3], planes[0]]

    def send_block(to, plane):
        remote(
            wnd.at[pl.ds(to * PAIRS, PAIRS)],
            wnd_recv.at[z, mine],
            d_send,
            d_recv.at[z],
            to,
            plane,
        ).start()

    @pl.loop(0, 4)
    def _(k):
        g = lax.rem(z + hop_of(k), 4)
        first_r = (64 + g * 16).astype(F32) + 2 * row_block
        for half in range(2):
            pick = (lane.astype(F32) == first_r + half).astype(F32).astype(BF16)
            of_row = lax.dot_general(pick, proj, NT, preferred_element_type=F32)
            lhs[:, pl.ds(half * SHARE, SHARE)] = (onehot * of_row).astype(BF16)
        sums = jnp.dot(lhs[...], rhs[...], preferred_element_type=F32)
        wnd[pl.ds(g * 8 * PAIRS, 8 * PAIRS)] = sums.astype(BF16).reshape(8 * PAIRS, 2, 128)

        @pl.loop(0, 3)
        def _(n):
            row = g * 8 + lax.rem(y + hop_of(n), 4) * 2
            for plane in far_planes:
                send_block(row + c, plane)
                send_block(row + 1 - c, plane)

        for plane in far_planes[:3]:
            send_block(g * 8 + y * 2 + c, plane)
            send_block(g * 8 + y * 2 + 1 - c, plane)
        send_block(g * 8 + y * 2 + 1 - c, pb)

        @pl.when(k < 3)
        def _():
            send_block(g * 8 + y * 2 + c, pb)

    wnd_recv[z, mine] = wnd[pl.ds(tok * PAIRS, PAIRS)]
    lane8 = lax.broadcasted_iota(jnp.int32, (8, 512), 1)
    row8 = lax.broadcasted_iota(jnp.int32, (8, 512), 0)
    first = jnp.broadcast_to(starts, (8, 512)) // SHARE
    last = jnp.where(lane8 == 511, DEVICES - 1, pltpu.roll(first, 511, 1))
    facts = jnp.where(row8 == 0, first.astype(F32), jnp.where(row8 == 1, last.astype(F32), doc_slot))
    rank = docs_ref[1] * 16 + lax.broadcasted_iota(jnp.int32, (1, 512), 1) // 32
    perm = (rank == lax.broadcasted_iota(jnp.int32, (512, 512), 0)).astype(F32).astype(BF16)
    ranked = lax.dot_general(perm, facts.astype(BF16), NT, preferred_element_type=F32)
    block, slot = split_slots(lax.broadcasted_iota(jnp.int32, (8, 32 * SLOTS), 1).astype(F32))
    block = block[0:1, :]
    own_slot = ranked[:, 2:3] == slot[0:1, :]

    @pl.loop(0, 4)
    def _(g):
        from_block = ranked[:, 0:1] - (g * 32).astype(F32)
        to_block = ranked[:, 1:2] - (g * 32).astype(F32)
        inside = (from_block <= block) & (block <= to_block) & own_slot
        place[g] = inside.astype(F32).astype(BF16)

    summed = jnp.zeros((512, 128), F32)
    for n in (2, 3, 1, 0):
        g = (z + n) % 4
        got = wnd_recv.at[g, pl.ds(0, (32 if n else 31) * PAIRS)]
        drain(got, d_recv.at[g])
        summed = summed + jnp.dot(
            place[g], wnd_recv[g].reshape(32 * SLOTS, 128), preferred_element_type=F32
        )
    units[...] = summed.astype(BF16).reshape(4, 4, 32, 128)

    at_y = pl.ds(pl.multiple_of(y * 128, 128), 128)
    at_z = pl.ds(pl.multiple_of(z * 128, 128), 128)
    def other(n, mine):
        return n + jnp.where(n >= mine, 1, 0)

    u_copies = []
    for n in range(3):
        ty, tz = other(n, y), other(n, z)
        u_copies.append(
            remote(
                units.at[:, ty], va.at[:, :, at_y], u_send, u_recv.at[0], z * 8 + ty * 2 + c, pb
            )
        )
        u_copies.append(
            remote(
                units.at[tz], vb.at[:, :, at_z], u_send, u_recv.at[1], tz * 8 + y * 2 + c, pb
            )
        )
    for copy in u_copies:
        copy.start()
    va[:, :, at_y] = units[:, y]
    vb[:, :, at_z] = units[z]
    fa_me, fb_me = z * 2 + c, y * 2 + c

    drain(q_all.at[0], qs_recv.at[1])
    for n in range(4):
        qa_t[pl.ds(n * 128, 128), :] = q_all[0, n].T
        qb_t[pl.ds(n * 128, 128), :] = q_all[1, n].T

    drain(va.at[:, :, pl.ds(0, 384)], u_recv.at[0])
    docs = va[...].reshape(128, 512)
    fa[:, :1024] = jnp.dot(docs, qa_t[...], preferred_element_type=F32).astype(BF16)
    wide = docs.astype(F32)
    square = jnp.broadcast_to(jnp.sum(wide * wide, axis=1, keepdims=True), (128, 128))
    high = square.astype(BF16).astype(F32)
    fa[:, 1024:] = jnp.where(
        lax.broadcasted_iota(jnp.int32, (128, 128), 1) < 64, high, square - high
    ).astype(BF16)

    @pl.loop(0, 7)
    def _(n):
        k = other(n, z * 2 + 1 - c)
        to = k + 1 - 2 * lax.rem(k, 2)
        remote(
            fa.at[pl.ds(pl.multiple_of(to * 16, 16), 16)],
            fa_recv.at[fa_me],
            f_send,
            f_recv.at[0],
            lax.div(to, 2) * 8 + y * 2 + lax.rem(to, 2),
            pb,
        ).start()

    drain(vb.at[:, :, pl.ds(0, 384)], u_recv.at[1])
    fb[...] = jnp.dot(vb[...].reshape(128, 512), qb_t[...], preferred_element_type=F32).astype(BF16)

    @pl.loop(0, 7)
    def _(n):
        k = other(n, y * 2 + 1 - c)
        to = k + 1 - 2 * lax.rem(k, 2)
        remote(
            fb.at[pl.ds(pl.multiple_of(to * 16, 16), 16)],
            fb_recv.at[fb_me],
            f_send,
            f_recv.at[1],
            z * 8 + to,
            pb,
        ).start()

    fa_recv[fa_me] = fa[pl.ds(pl.multiple_of(fa_me * 16, 16), 16), :]
    fb_recv[fb_me] = fb[pl.ds(pl.multiple_of(fb_me * 16, 16), 16), :]
    drain(fa_recv.at[pl.ds(0, 7)], f_recv.at[0])
    total_a = fa_recv[0].astype(F32)
    for n in range(1, 8):
        total_a = total_a + fa_recv[n].astype(F32)
    tail = total_a[:, 1024:]
    norm = lax.rsqrt(tail + pltpu.roll(tail, 64, 1) + EPS)[:, 0:1]
    out_ref[:, :1024] = total_a[:, :1024] * norm
    drain(fb_recv.at[pl.ds(0, 7)], f_recv.at[1])
    total_b = fb_recv[0].astype(F32)
    for n in range(1, 8):
        total_b = total_b + fb_recv[n].astype(F32)
    out_ref[:, 1024:] = total_b * norm

    drain(proj_send, p_send)
    drain(q_all.at[:, pl.ds(0, 3)], qs_send)
    for n in range(2):
        drain(va.at[:, :, pl.ds(0, 384)], u_send)
    for g in range(4):
        drain(wnd.at[pl.ds(0, (32 if g else 31) * PAIRS)], d_send)
    drain(fa.at[pl.ds(0, 112)], f_send)
    drain(fb.at[pl.ds(0, 112)], f_send)


def per_device(activations, out_grads, proj_in, proj_out, doc_starts, doc_owner, queries):
    depth_in, depth_out = activations.shape[1], out_grads.shape[1]
    dma = pltpu.SemaphoreType.DMA
    vmem = pltpu.VMEM

    def on_hbm(array):
        return pltpu.with_memory_space_constraint(array, pltpu.HBM)

    return pl.pallas_call(
        kernel,
        out_shape=jax.ShapeDtypeStruct((16, 2048), F32),
        in_specs=[pl.BlockSpec(memory_space=pltpu.HBM)] * 7,
        out_specs=pl.BlockSpec(memory_space=pltpu.VMEM),
        scratch_shapes=[
            vmem((4, SHARE, depth_in + depth_out), BF16),
            vmem((128, depth_in + depth_out), BF16),
            vmem((2, 1, 512), jnp.int32),
            vmem((3, SHARE, 128), BF16),
            vmem((SHARE, 128), F32),
            vmem((2, SHARE, 128), BF16),
            vmem((SHARE, 128), BF16),
            vmem((GROUP, SHARE), F32),
            vmem((4, 512, 32 * SLOTS), BF16),
            vmem((GROUP, 2 * SHARE), BF16),
            vmem((2 * SHARE, 128), BF16),
            vmem((32 * PAIRS, 2, 128), BF16),
            vmem((4, 32 * PAIRS, 2, 128), BF16),
            vmem((4, 4, 32, 128), BF16),
            vmem((4, 32, 512), BF16),
            vmem((4, 32, 512), BF16),
            vmem((2, 4, 1024, 128), BF16),
            vmem((512, 1024), BF16),
            vmem((512, 1024), BF16),
            vmem((128, 1152), BF16),
            vmem((128, 1024), BF16),
            vmem((8, 16, 1152), BF16),
            vmem((8, 16, 1024), BF16),
            dma((5,)),
            dma,
            dma,
            dma,
            dma,
            dma((2,)),
            dma,
            dma,
            dma,
            dma,
            dma((4,)),
            dma,
            dma((2,)),
            dma,
            dma((2,)),
            pltpu.SemaphoreType.REGULAR((3,)),
        ],
        compiler_params=pltpu.CompilerParams(
            collective_id=0, has_side_effects=True, vmem_limit_bytes=48 * 1024 * 1024
        ),
    )(
        on_hbm(activations),
        on_hbm(out_grads),
        on_hbm(proj_in.T),
        on_hbm(proj_out.T),
        on_hbm(doc_starts.reshape(1, 512)),
        on_hbm(doc_owner.reshape(1, 512)),
        on_hbm(queries),
    )


def solution(mesh):
    in_specs = (
        P("tok", "pb"),
        P("tok", "pb"),
        P("pb", None),
        P("pb", None),
        P(),
        P(),
        P("pb", "tok"),
    )
    return jax.shard_map(
        per_device, mesh=mesh, in_specs=in_specs, out_specs=P("tok", "pb"), check_vma=False
    )
```

```python
import functools

import jax
import jax.numpy as jnp
from jax import lax
from jax.experimental import pallas as pl
from jax.experimental.pallas import tpu as pltpu
from jax.sharding import PartitionSpec as P

EPS = 1e-06
SHARE = 512
SLOTS = 10
PAIRS = SLOTS // 2
GROUP = 8 * SLOTS
MESH = pl.DeviceIdType.MESH
DEVICES = 128
HALF = 256
NT = (((1,), (1,)), ((), ()))
F32 = jnp.float32
BF16 = jnp.bfloat16


def remote(src, dst, send_sem, recv_sem, tok, pb):
    return pltpu.make_async_remote_copy(
        src_ref=src,
        dst_ref=dst,
        send_sem=send_sem,
        recv_sem=recv_sem,
        device_id=(tok, pb),
        device_id_type=MESH,
    )


def drain(ref, sem):
    pltpu.make_async_copy(ref, ref, sem).wait()


def split_slots(numbers):
    quotient = jnp.floor((numbers + 0.5) * (1.0 / SLOTS))
    return quotient, numbers - SLOTS * quotient


def hop_of(t):
    return jnp.where(t == 0, 2, jnp.where(t == 1, 1, jnp.where(t == 2, 3, 0)))


def kernel(
    act_hbm,
    grad_hbm,
    win_hbm,
    wout_hbm,
    starts_hbm,
    owner_hbm,
    q_hbm,
    out_ref,
    tokens,
    weights,
    docs_ref,
    proj_send,
    proj_own,
    proj_recv,
    proj_relay,
    onehot_ref,
    place,
    lhs,
    rhs,
    wnd,
    wnd_recv,
    units,
    va,
    vb,
    q_all,
    qa_t,
    qb_t,
    fa,
    fb,
    fa_recv,
    fb_recv,
    load_sem,
    w_sem,
    docs_sem,
    q_sem,
    qs_send,
    qs_recv,
    p_send,
    relay_recv,
    p_recv,
    d_send,
    d_recv,
    u_send,
    u_recv,
    f_send,
    f_recv,
    round_sem,
):
    tok = lax.axis_index("tok")
    pb = lax.axis_index("pb")
    z, y, c = tok // 8, (tok // 2) % 4, tok % 2
    me = tok * 4 + pb

    depth_in = act_hbm.shape[1]
    depth_out = grad_hbm.shape[1]
    of_act, of_grad = pl.ds(0, depth_in), pl.ds(depth_in, depth_out)

    def loads_of(hop, half, t, at, sem):
        rows = pl.ds(pl.multiple_of(lax.rem(pb + hop, 4) * SHARE + half * HALF, HALF), HALF)
        return [
            pltpu.make_async_copy(grad_hbm.at[rows], tokens.at[t, at, of_grad], load_sem.at[sem]),
            pltpu.make_async_copy(act_hbm.at[rows], tokens.at[t, at, of_act], load_sem.at[sem]),
        ]

    def far_half(s):
        return pl.ds(pl.multiple_of(s * HALF, HALF), HALF)

    first_half, second_half = pl.ds(0, HALF), pl.ds(HALF, HALF)

    def full_loads(t):
        return loads_of(jnp.where(t == 3, 0, 1), jnp.where(t == 1, 1, 0), t, first_half, t + 1) + loads_of(
            jnp.where(t == 3, 0, 3), jnp.where(t == 1, 0, 1), t, second_half, t + 1
        )

    small = [
        pltpu.make_async_copy(wout_hbm, weights.at[pl.ds(64, 64), of_grad], w_sem),
        pltpu.make_async_copy(win_hbm, weights.at[pl.ds(0, 64), of_act], w_sem),
        pltpu.make_async_copy(starts_hbm, docs_ref.at[0], docs_sem),
        pltpu.make_async_copy(owner_hbm, docs_ref.at[1], docs_sem),
    ]
    q_loads = [
        pltpu.make_async_copy(q_hbm.at[pl.ds(0, 1024)], q_all.at[0, y], q_sem),
        pltpu.make_async_copy(q_hbm.at[pl.ds(1024, 1024)], q_all.at[1, z], q_sem),
    ]
    small[0].start()
    small[1].start()
    for copy in loads_of(2, 0, 0, first_half, 0) + q_loads + loads_of(2, 1, 0, second_half, 1):
        copy.start()

    @pl.loop(1, 4)
    def _(t):
        for copy in full_loads(t):
            copy.start()

    small[2].start()
    small[3].start()

    planes = [lax.rem(pb + n, 4) for n in range(4)]
    on_y = [z * 8 + lax.rem(y + n, 4) * 2 + c for n in range(1, 4)]
    on_z = [lax.rem(z + n, 4) * 8 + y * 2 + c for n in range(1, 4)]
    on_core = [z * 8 + y * 2 + 1 - c]

    def signal(sem, toks):
        for to in toks:
            pl.semaphore_signal(sem, inc=1, device_id=(to, pb), device_id_type=MESH)

    barrier = pltpu.get_barrier_semaphore()
    for plane in planes[1:]:
        pl.semaphore_signal(barrier, inc=1, device_id=(tok, plane), device_id_type=MESH)
    signal(barrier, on_y + on_z + on_core)

    q_first, q_second, q_passed = [], [], []
    for h, place_me in enumerate((y, z)):
        right, left = lax.rem(place_me + 1, 4), lax.rem(place_me + 3, 4)
        for k, (to, row, src, group) in enumerate(
            (
                (right, 0, place_me, q_first),
                (left, 512, place_me, q_first),
                (right, 512, place_me, q_second),
                (left, 0, place_me, q_second),
                (right, 0, left, q_passed),
                (left, 512, right, q_passed),
            )
        ):
            part = q_all.at[h, src, pl.ds(row, 512)]
            to_tok = z * 8 + to * 2 + c if h == 0 else to * 8 + y * 2 + c
            group.append(remote(part, part, qs_send, qs_recv.at[0 if k < 2 else 1], to_tok, pb))

    weights[:64, depth_in:] = jnp.zeros((64, depth_out), BF16)
    weights[64:, :depth_in] = jnp.zeros((64, depth_in), BF16)
    drain(weights.at[pl.ds(0, 64)], w_sem)

    def project(t, at):
        return lax.dot_general(tokens[t, at, :], weights[...], NT, preferred_element_type=F32)

    def relay_copy(s):
        return remote(
            proj_send.at[0, far_half(s)],
            proj_relay.at[far_half(s)],
            p_send,
            relay_recv,
            tok,
            lax.rem(pb + 2, 4),
        )

    def proj_copies(t):
        return [
            remote(
                proj_send.at[t, at],
                proj_recv.at[n, pl.ds(pl.multiple_of(half * HALF, HALF), HALF)],
                p_send,
                p_recv,
                tok,
                lax.rem(pb + 1 + 2 * n, 4),
            )
            for n, at, half in ((0, first_half, 2 - t), (1, second_half, t - 1))
        ]

    @pl.loop(0, 2)
    def _(s):
        drain(tokens.at[0, far_half(s)], load_sem.at[s])
        proj_send[0, far_half(s), :] = project(0, far_half(s)).astype(BF16)

        @pl.when(s == 0)
        def _():
            pl.semaphore_wait(barrier, 10)
            signal(round_sem.at[0], on_y)

        relay_copy(s).start()

        @pl.when(s == 0)
        def _():
            drain(q_all.at[0, pl.ds(0, 2)], q_sem)
            for copy in q_first + q_second:
                copy.start()

    @pl.loop(1, 4)
    def _(t):
        drain(tokens.at[t], load_sem.at[t + 1])
        both = project(t, pl.ds(0, SHARE))

        @pl.when(t < 3)
        def _():
            proj_send[t] = both.astype(BF16)
            for copy in proj_copies(t):
                copy.start()

        @pl.when(t == 1)
        def _():
            pl.semaphore_wait(round_sem.at[0], 3)
            signal(round_sem.at[1], on_z)

        @pl.when(t == 2)
        def _():
            pl.semaphore_wait(round_sem.at[1], 3)
            signal(round_sem.at[2], on_core)

        @pl.when(t == 3)
        def _():
            proj_own[...] = both

    pl.semaphore_wait(round_sem.at[2], 1)
    drain(q_all.at[0, pl.ds(0, 2)], qs_recv.at[0])
    for copy in q_passed:
        copy.start()

    drain(docs_ref, docs_sem)
    starts = docs_ref[0]
    begun = starts <= me * SHARE + lax.broadcasted_iota(jnp.int32, (SHARE, 512), 0)
    doc = lax.broadcasted_iota(jnp.int32, (8, 512), 1).astype(F32)
    doc_slot = split_slots(doc)[1]
    slot_before = jnp.where(doc > 0, split_slots(doc - 1)[1], -1.0)
    row_block, row_slot = split_slots(lax.broadcasted_iota(jnp.int32, (GROUP, 128), 0).astype(F32))
    slot_row = row_slot[:, 0:1]
    enters = (doc_slot[0:1, :] == slot_row).astype(F32) - (slot_before[0:1, :] == slot_row).astype(F32)
    onehot_ref[...] = lax.dot_general(
        enters.astype(BF16), begun.astype(F32).astype(BF16), NT, preferred_element_type=F32
    )

    drain(proj_relay, relay_recv)
    proj = proj_own[...] + proj_relay[...].astype(F32)
    drain(proj_recv, p_recv)
    for t in range(2):
        proj = proj + proj_recv[t].astype(F32)
    proj = proj.astype(BF16)

    onehot = onehot_ref[...]
    lane = lax.broadcasted_iota(jnp.int32, (GROUP, 128), 1)
    low = lax.broadcasted_iota(jnp.int32, (SHARE, 128), 1) < 64
    wide = proj.astype(F32)
    rhs[...] = jnp.concatenate(
        [jnp.where(low, wide, 0.0), jnp.where(low, 0.0, pltpu.roll(wide, 64, 1))], axis=0
    ).astype(BF16)
    mine = pl.ds(lax.rem(me, 32) * PAIRS, PAIRS)

    def send_block(to, plane):
        remote(
            wnd.at[pl.ds(to * PAIRS, PAIRS)],
            wnd_recv.at[z, mine],
            d_send,
            d_recv.at[z],
            to,
            plane,
        ).start()

    @pl.loop(0, 4)
    def _(k):
        g = lax.rem(z + hop_of(k), 4)
        first_r = (64 + g * 16).astype(F32) + 2 * row_block
        for half in range(2):
            pick = (lane.astype(F32) == first_r + half).astype(F32).astype(BF16)
            of_row = lax.dot_general(pick, proj, NT, preferred_element_type=F32)
            lhs[:, pl.ds(half * SHARE, SHARE)] = (onehot * of_row).astype(BF16)
        sums = jnp.dot(lhs[...], rhs[...], preferred_element_type=F32)
        wnd[pl.ds(g * 8 * PAIRS, 8 * PAIRS)] = sums.astype(BF16).reshape(8 * PAIRS, 2, 128)

        @pl.loop(0, 3)
        def _(n):
            row = g * 8 + lax.rem(y + hop_of(n), 4) * 2
            for plane in range(4):
                send_block(row + c, plane)
                send_block(row + 1 - c, plane)

        for plane in range(4):
            send_block(g * 8 + y * 2 + 1 - c, plane)

            @pl.when((k < 3) | (pb != plane))
            def _():
                send_block(g * 8 + y * 2 + c, plane)

    wnd_recv[z, mine] = wnd[pl.ds(tok * PAIRS, PAIRS)]
    lane8 = lax.broadcasted_iota(jnp.int32, (8, 512), 1)
    row8 = lax.broadcasted_iota(jnp.int32, (8, 512), 0)
    first = jnp.broadcast_to(starts, (8, 512)) // SHARE
    last = jnp.where(lane8 == 511, DEVICES - 1, pltpu.roll(first, 511, 1))
    facts = jnp.where(row8 == 0, first.astype(F32), jnp.where(row8 == 1, last.astype(F32), doc_slot))
    rank = docs_ref[1] * 16 + lax.broadcasted_iota(jnp.int32, (1, 512), 1) // 32
    perm = (rank == lax.broadcasted_iota(jnp.int32, (512, 512), 0)).astype(F32).astype(BF16)
    ranked = lax.dot_general(perm, facts.astype(BF16), NT, preferred_element_type=F32)
    block, slot = split_slots(lax.broadcasted_iota(jnp.int32, (8, 32 * SLOTS), 1).astype(F32))
    block = block[0:1, :]
    own_slot = ranked[:, 2:3] == slot[0:1, :]

    @pl.loop(0, 4)
    def _(g):
        from_block = ranked[:, 0:1] - (g * 32).astype(F32)
        to_block = ranked[:, 1:2] - (g * 32).astype(F32)
        inside = (from_block <= block) & (block <= to_block) & own_slot
        place[g] = inside.astype(F32).astype(BF16)

    summed = jnp.zeros((512, 128), F32)
    for n in (2, 3, 1, 0):
        g = (z + n) % 4
        got = wnd_recv.at[g, pl.ds(0, (32 if n else 31) * PAIRS)]
        drain(got, d_recv.at[g])
        summed = summed + jnp.dot(
            place[g], wnd_recv[g].reshape(32 * SLOTS, 128), preferred_element_type=F32
        )
    units[...] = summed.astype(BF16).reshape(4, 4, 32, 128)

    at_y = pl.ds(pl.multiple_of(y * 128, 128), 128)
    at_z = pl.ds(pl.multiple_of(z * 128, 128), 128)
    def other(n, mine):
        return n + jnp.where(n >= mine, 1, 0)

    u_copies = []
    for n in range(3):
        ty, tz = other(n, y), other(n, z)
        u_copies.append(
            remote(
                units.at[:, ty], va.at[:, :, at_y], u_send, u_recv.at[0], z * 8 + ty * 2 + c, pb
            )
        )
        u_copies.append(
            remote(
                units.at[tz], vb.at[:, :, at_z], u_send, u_recv.at[1], tz * 8 + y * 2 + c, pb
            )
        )
    for copy in u_copies:
        copy.start()
    va[:, :, at_y] = units[:, y]
    vb[:, :, at_z] = units[z]
    fa_me, fb_me = z * 2 + c, y * 2 + c

    drain(q_all.at[0], qs_recv.at[1])
    for n in range(4):
        qa_t[pl.ds(n * 128, 128), :] = q_all[0, n].T
        qb_t[pl.ds(n * 128, 128), :] = q_all[1, n].T

    drain(va.at[:, :, pl.ds(0, 384)], u_recv.at[0])
    docs = va[...].reshape(128, 512)
    fa[:, :1024] = jnp.dot(docs, qa_t[...], preferred_element_type=F32).astype(BF16)
    wide = docs.astype(F32)
    square = jnp.broadcast_to(jnp.sum(wide * wide, axis=1, keepdims=True), (128, 128))
    high = square.astype(BF16).astype(F32)
    fa[:, 1024:] = jnp.where(
        lax.broadcasted_iota(jnp.int32, (128, 128), 1) < 64, high, square - high
    ).astype(BF16)

    @pl.loop(0, 7)
    def _(n):
        k = other(n, z * 2 + 1 - c)
        to = k + 1 - 2 * lax.rem(k, 2)
        remote(
            fa.at[pl.ds(pl.multiple_of(to * 16, 16), 16)],
            fa_recv.at[fa_me],
            f_send,
            f_recv.at[0],
            lax.div(to, 2) * 8 + y * 2 + lax.rem(to, 2),
            pb,
        ).start()

    drain(vb.at[:, :, pl.ds(0, 384)], u_recv.at[1])
    fb[...] = jnp.dot(vb[...].reshape(128, 512), qb_t[...], preferred_element_type=F32).astype(BF16)

    @pl.loop(0, 7)
    def _(n):
        k = other(n, y * 2 + 1 - c)
        to = k + 1 - 2 * lax.rem(k, 2)
        remote(
            fb.at[pl.ds(pl.multiple_of(to * 16, 16), 16)],
            fb_recv.at[fb_me],
            f_send,
            f_recv.at[1],
            z * 8 + to,
            pb,
        ).start()

    fa_recv[fa_me] = fa[pl.ds(pl.multiple_of(fa_me * 16, 16), 16), :]
    fb_recv[fb_me] = fb[pl.ds(pl.multiple_of(fb_me * 16, 16), 16), :]
    drain(fa_recv.at[pl.ds(0, 7)], f_recv.at[0])
    total_a = fa_recv[0].astype(F32)
    for n in range(1, 8):
        total_a = total_a + fa_recv[n].astype(F32)
    tail = total_a[:, 1024:]
    norm = lax.rsqrt(tail + pltpu.roll(tail, 64, 1) + EPS)[:, 0:1]
    out_ref[:, :1024] = total_a[:, :1024] * norm
    drain(fb_recv.at[pl.ds(0, 7)], f_recv.at[1])
    total_b = fb_recv[0].astype(F32)
    for n in range(1, 8):
        total_b = total_b + fb_recv[n].astype(F32)
    out_ref[:, 1024:] = total_b * norm

    drain(proj_send, p_send)
    drain(q_all.at[:, pl.ds(0, 3)], qs_send)
    for n in range(2):
        drain(va.at[:, :, pl.ds(0, 384)], u_send)
    for g in range(4):
        drain(wnd.at[pl.ds(0, (32 if g else 31) * PAIRS)], d_send)
    drain(fa.at[pl.ds(0, 112)], f_send)
    drain(fb.at[pl.ds(0, 112)], f_send)


def per_device(activations, out_grads, proj_in, proj_out, doc_starts, doc_owner, queries):
    depth_in, depth_out = activations.shape[1], out_grads.shape[1]
    dma = pltpu.SemaphoreType.DMA
    vmem = pltpu.VMEM

    def on_hbm(array):
        return pltpu.with_memory_space_constraint(array, pltpu.HBM)

    return pl.pallas_call(
        kernel,
        out_shape=jax.ShapeDtypeStruct((16, 2048), F32),
        in_specs=[pl.BlockSpec(memory_space=pltpu.HBM)] * 7,
        out_specs=pl.BlockSpec(memory_space=pltpu.VMEM),
        scratch_shapes=[
            vmem((4, SHARE, depth_in + depth_out), BF16),
            vmem((128, depth_in + depth_out), BF16),
            vmem((2, 1, 512), jnp.int32),
            vmem((3, SHARE, 128), BF16),
            vmem((SHARE, 128), F32),
            vmem((2, SHARE, 128), BF16),
            vmem((SHARE, 128), BF16),
            vmem((GROUP, SHARE), F32),
            vmem((4, 512, 32 * SLOTS), BF16),
            vmem((GROUP, 2 * SHARE), BF16),
            vmem((2 * SHARE, 128), BF16),
            vmem((32 * PAIRS, 2, 128), BF16),
            vmem((4, 32 * PAIRS, 2, 128), BF16),
            vmem((4, 4, 32, 128), BF16),
            vmem((4, 32, 512), BF16),
            vmem((4, 32, 512), BF16),
            vmem((2, 4, 1024, 128), BF16),
            vmem((512, 1024), BF16),
            vmem((512, 1024), BF16),
            vmem((128, 1152), BF16),
            vmem((128, 1024), BF16),
            vmem((8, 16, 1152), BF16),
            vmem((8, 16, 1024), BF16),
            dma((5,)),
            dma,
            dma,
            dma,
            dma,
            dma((2,)),
            dma,
            dma,
            dma,
            dma,
            dma((4,)),
            dma,
            dma((2,)),
            dma,
            dma((2,)),
            pltpu.SemaphoreType.REGULAR((3,)),
        ],
        compiler_params=pltpu.CompilerParams(
            collective_id=0, has_side_effects=True, vmem_limit_bytes=48 * 1024 * 1024
        ),
    )(
        on_hbm(activations),
        on_hbm(out_grads),
        on_hbm(proj_in.T),
        on_hbm(proj_out.T),
        on_hbm(doc_starts.reshape(1, 512)),
        on_hbm(doc_owner.reshape(1, 512)),
        on_hbm(queries),
    )


def solution(mesh):
    in_specs = (
        P("tok", "pb"),
        P("tok", "pb"),
        P("pb", None),
        P("pb", None),
        P(),
        P(),
        P("pb", "tok"),
    )
    return jax.shard_map(
        per_device, mesh=mesh, in_specs=in_specs, out_specs=P("tok", "pb"), check_vma=False
    )
```
